32 devices in a mesh: seq: 8 (over y, x, core), head: 4 (over z).
Axes of the slice: x: 2, y: 2, z: 4, core: 2. Of those that a mesh axis runs over, the one named last changes fastest.
Arguments:
- queries: bfloat16 [1024, 2048], P('seq', 'head'), may hold values from -150 to 150
- keys: bfloat16 [1024, 1024], P('seq', 'head'), may hold values from -5 to 5
- values: bfloat16 [1024, 1024], P('seq', 'head'), may hold values from -5 to 5
- prefix_resid: bfloat16 [1024, 5376], P('seq', 'head'), may hold values from -6 to 6
- opt_queries: bfloat16 [8, 64, 2048], P('seq', None, 'head'), may hold values from -150 to 150
- opt_keys: bfloat16 [8, 64, 1024], P('seq', None, 'head'), may hold values from -5 to 5
- opt_values: bfloat16 [8, 64, 1024], P('seq', None, 'head'), may hold values from -5 to 5
- opt_resid: bfloat16 [8, 64, 5376], P('seq', None, 'head'), may hold values from -6 to 6
- out_weight: bfloat16 [2048, 5376], P('seq', 'head'), may hold values from -0.5347495 to 0.5347495
- norm_gain: float32 [5376], P('head'), may hold values from 0.1 to 1.9
- option_bounds: int32 [8, 2], P('seq'), may hold values from 0 to 64, as said below
Outputs:
- prefix_out: bfloat16 [1024, 5376], P('seq', 'head')
- option_out: bfloat16 [8, 64, 5376], P('seq', None, 'head')
- option_summary: float32 [8, 5376], P('seq', 'head')
The draws below stay inside these ranges and needn't reach their ends.
Inputs may be any that keep to these rules, and one draw needn't show every extreme that they name: `option_bounds`: column 0 is an option's first answer position and column 1 its length, with 0 <= start < length; some option has length 64.
All inputs are finite; a program needn't handle non-finite values.
Results may differ from the reference program's by a relative error of at most 0.009.
Values may be sent and summed in bfloat16 or wider, within the bound.
No kernel may reach another device: no remote copies, remote signals or barrier semaphores. Data moves between devices by JAX's collectives and lax.ppermute only.
A program may use at most 64 MiB of HBM per device.

```python
import jax
import jax.numpy as jnp
from jax import lax

D = 5376
HQ = 16
KVH = 8
HD = 128
WINDOW = 1024
TOK_DEV = 128
OPT_LEN = 64
TOKENS = 1024
OPTIONS = 8
N_HEAD = 4


def drawn_keys(key):
    base_key = jax.random.fold_in(key, 101)
    first_key = jax.random.fold_in(base_key, 0)
    keys_all = jnp.clip(jax.random.normal(first_key, (TOKENS, KVH * HD), jnp.float32), -5.0, 5.0)
    return keys_all


def draw_keys(key, part):
    return drawn_keys(key).astype(jnp.bfloat16)


def draw_queries(key, part):
    result = jnp.clip(jax.random.normal(jax.random.fold_in(key, 202), (TOKENS, HQ * HD), jnp.float32), -5.0, 5.0)
    return result.astype(jnp.bfloat16)


def draw_opt_queries(key, part):
    result = jnp.clip(jax.random.normal(jax.random.fold_in(key, 303), (OPTIONS, OPT_LEN, HQ * HD), jnp.float32), -5.0, 5.0)
    return result.astype(jnp.bfloat16)


def draw_out_weight(key, part):
    first_key, second_key = jax.random.split(jax.random.fold_in(key, 404), 2)
    base = jnp.clip(jax.random.normal(first_key, (HQ * HD, D), jnp.float32), -4.0, 4.0)
    column_pos = jnp.arange(D, dtype=jnp.float32) / (D - 1)
    column_scale = 3.0 ** column_pos * jnp.exp(jax.random.uniform(second_key, (D,), jnp.float32, -0.7, 0.7))
    return (base * column_scale[None, :] / jnp.sqrt(jnp.float32(HQ * HD))).astype(jnp.bfloat16)


def draw_option_bounds(key, part):
    first_key, second_key, third_key = jax.random.split(jax.random.fold_in(key, 505), 3)
    length = jax.random.randint(first_key, (OPTIONS,), 1, OPT_LEN + 1)
    longest = jax.random.randint(second_key, (), 0, OPTIONS)
    length = length.at[longest].set(OPT_LEN)
    start_pos = jax.random.randint(third_key, (OPTIONS,), 0, OPT_LEN) % length
    return jnp.stack([start_pos, length], axis=1).astype(jnp.int32)


def steps_of(key, shape, cuts, smallest, largest):
    gain = 1.0
    for position, shards_of in cuts:
        draws = jax.random.uniform(jax.random.fold_in(jax.random.fold_in(key, 6), position), (shards_of,), jnp.float32, smallest / len(cuts), largest / len(cuts))
        gain = gain * jnp.repeat(jnp.exp(draws), shape[position] // shards_of).reshape((-1,) + (1,) * (len(shape) - 1 - position))
    return gain


def normal_values(rng, shape, scale, reach, cuts=(), kind=jnp.bfloat16):
    values = scale * jax.random.normal(rng, shape, jnp.float32)
    if cuts:
        values = values * steps_of(rng, shape, cuts, -0.22, 0.18)
    return jnp.clip(values, -reach, reach).astype(kind)


def setup_inputs(seed: int = 0) -> dict:
    arg_keys = jax.random.split(jax.random.key(seed), 12)
    return {
        "queries": draw_queries(jax.random.fold_in(arg_keys[11], 71), 0),
        "keys": draw_keys(jax.random.fold_in(arg_keys[11], 71), 0),
        "values": normal_values(arg_keys[2], (TOKENS, KVH * HD), 1.0, 5.0, ((0, 8), (1, 4))),
        "prefix_resid": normal_values(arg_keys[3], (TOKENS, D), 1.0, 6.0, ((0, 8), (1, 4))),
        "opt_queries": draw_opt_queries(jax.random.fold_in(arg_keys[11], 71), 0),
        "opt_keys": normal_values(arg_keys[5], (OPTIONS, OPT_LEN, KVH * HD), 1.0, 5.0, ((0, 8), (2, 4))),
        "opt_values": normal_values(arg_keys[6], (OPTIONS, OPT_LEN, KVH * HD), 1.0, 5.0, ((0, 8), (2, 4))),
        "opt_resid": normal_values(arg_keys[7], (OPTIONS, OPT_LEN, D), 1.0, 6.0, ((0, 8), (2, 4))),
        "out_weight": draw_out_weight(jax.random.fold_in(arg_keys[11], 71), 0),
        "norm_gain": jnp.clip(1.0 + 0.18 * jax.random.normal(arg_keys[9], (D,), jnp.float32), 0.1, 1.9),
        "option_bounds": draw_option_bounds(jax.random.fold_in(arg_keys[11], 71), 0),
    }


score_scale = 168.0 ** (-0.5)
epsilon = 1e-06

def attend(query_rows, key_rows, value_rows, allowed):
    row_count = query_rows.shape[0]
    kv_heads = key_rows.shape[1] // HD
    groups = query_rows.shape[1] // key_rows.shape[1]
    query_view = query_rows.astype(jnp.float32).reshape(row_count, kv_heads, groups, HD)
    key_view = key_rows.astype(jnp.float32).reshape(-1, kv_heads, HD)
    scores = jnp.einsum('rkgd,lkd->kgrl', query_view, key_view) * score_scale
    scores = jnp.where(allowed[None, None], scores, -jnp.inf)
    row_max = lax.optimization_barrier(jnp.max(scores, axis=-1, keepdims=True))
    weights = jnp.exp(scores - row_max)
    weights = (weights / lax.optimization_barrier(jnp.sum(weights, axis=-1, keepdims=True))).astype(jnp.bfloat16)
    value_view = value_rows.astype(jnp.float32).reshape(-1, kv_heads, HD)
    attended = jnp.einsum('kgrl,lkd->rkgd', weights.astype(jnp.float32), value_view)
    return attended.reshape(row_count, -1).astype(jnp.bfloat16)

def project_norm(stacked, out_weight, norm_gain):
    head_cols = HQ * HD // N_HEAD
    projected = jnp.zeros((stacked.shape[0], D), jnp.float32)
    for group in range(N_HEAD):
        partial_value = jnp.dot(stacked[:, group * head_cols:(group + 1) * head_cols], out_weight[group * head_cols:(group + 1) * head_cols], preferred_element_type=jnp.float32)
        projected = projected + lax.optimization_barrier(partial_value.astype(jnp.bfloat16)).astype(jnp.float32)
    mean_square = lax.optimization_barrier(jnp.mean(projected * projected, axis=-1, keepdims=True))
    return projected * lax.rsqrt(mean_square + epsilon) * norm_gain.astype(jnp.float32)

def reference(queries, keys, values, prefix_resid, opt_queries, opt_keys, opt_values, opt_resid, out_weight, norm_gain, option_bounds):
    padded_keys = jnp.concatenate([jnp.zeros((WINDOW, keys.shape[1]), keys.dtype), keys], axis=0)
    padded_values = jnp.concatenate([jnp.zeros((WINDOW, values.shape[1]), values.dtype), values], axis=0)

    def prefix_block(block_index):
        first_row = block_index * TOK_DEV
        block_queries = lax.dynamic_slice_in_dim(queries, first_row, TOK_DEV, 0)
        block_keys = lax.dynamic_slice_in_dim(padded_keys, first_row, WINDOW + TOK_DEV, 0)
        block_values = lax.dynamic_slice_in_dim(padded_values, first_row, WINDOW + TOK_DEV, 0)
        query_pos = first_row + jnp.arange(TOK_DEV, dtype=jnp.int32)
        key_pos = first_row - WINDOW + jnp.arange(WINDOW + TOK_DEV, dtype=jnp.int32)
        allowed = (key_pos[None] <= query_pos[:, None]) & (key_pos[None] > query_pos[:, None] - WINDOW) & (key_pos[None] >= 0)
        return attend(block_queries, block_keys, block_values, allowed)
    prefix_attn = lax.map(prefix_block, jnp.arange(TOKENS // TOK_DEV, dtype=jnp.int32)).reshape(TOKENS, -1)
    last_keys = keys[TOKENS - WINDOW:]
    last_values = values[TOKENS - WINDOW:]
    positions = jnp.arange(WINDOW + OPT_LEN, dtype=jnp.int32)
    option_pos = jnp.arange(OPT_LEN, dtype=jnp.int32)
    option_allowed = jnp.where(positions[None] < WINDOW, positions[None] > option_pos[:, None], positions[None] - WINDOW <= option_pos[:, None])

    def option_block(inputs):
        option_queries, own_keys, own_values = inputs
        joined_keys = jnp.concatenate([last_keys, own_keys], axis=0)
        joined_values = jnp.concatenate([last_values, own_values], axis=0)
        return attend(option_queries, joined_keys, joined_values, option_allowed)
    option_attn = lax.map(option_block, (opt_queries, opt_keys, opt_values)).reshape(OPTIONS * OPT_LEN, -1)
    prefix_normed = project_norm(prefix_attn, out_weight, norm_gain)
    option_normed = project_norm(option_attn, out_weight, norm_gain)
    prefix_out = (prefix_resid.astype(jnp.float32) + prefix_normed).astype(jnp.bfloat16)
    option_full = opt_resid.astype(jnp.float32) + option_normed.reshape(OPTIONS, OPT_LEN, D)
    start_pos = option_bounds[:, 0]
    length = option_bounds[:, 1]
    inside = option_pos[None, :] < length[:, None]
    option_out = jnp.where(inside[:, :, None], option_full, 0.0).astype(jnp.bfloat16)
    chosen = inside & (option_pos[None, :] >= start_pos[:, None])
    option_summary = lax.optimization_barrier(jnp.sum(jnp.where(chosen[:, :, None], option_out.astype(jnp.float32), 0.0), axis=1)) / (length - start_pos).astype(jnp.float32)[:, None]
    return (prefix_out, option_out, option_summary)
```

```python
import functools

import jax
import jax.numpy as jnp
from jax import lax
from jax.experimental import pallas as pl
from jax.experimental.pallas import tpu as pltpu
from jax.sharding import PartitionSpec as P

HD = 128
WINDOW = 1024
score_scale = 168.0 ** (-0.5)
exp2_scale = score_scale * 1.4426950408889634
epsilon = 1e-06
VMEM_BYTES = 40 * 1024 * 1024


def passed_along(value, axis, steps):
    count = lax.axis_size(axis)
    initial, last = (max(0, -steps), min(count, count - steps))
    return lax.ppermute(value, axis, [(source, source + steps) for source in range(initial, last)])


def from_root(block, axis, owner):
    block = jnp.where(lax.axis_index(axis) == owner, block, jnp.zeros_like(block))
    return lax.psum(block, axis)


def attend(query_rows, key_rows, value_rows, allowed):
    row_count = query_rows.shape[0]
    kv_heads = key_rows.shape[1] // HD
    groups = query_rows.shape[1] // key_rows.shape[1]
    query_view = query_rows.reshape(row_count, kv_heads, groups, HD)
    key_view = key_rows.reshape(-1, kv_heads, HD)
    scores = (
        jnp.einsum("rkgd,lkd->kgrl", query_view, key_view, preferred_element_type=jnp.float32)
        * score_scale
    )
    scores = jnp.where(allowed[None, None], scores, -jnp.inf)
    row_max = jnp.max(scores, axis=-1, keepdims=True)
    weights = jnp.exp(scores - row_max)
    weights = (weights / jnp.sum(weights, axis=-1, keepdims=True)).astype(jnp.bfloat16)
    value_view = value_rows.reshape(-1, kv_heads, HD)
    attended = jnp.einsum("kgrl,lkd->rkgd", weights, value_view, preferred_element_type=jnp.float32)
    return attended.reshape(row_count, -1).astype(jnp.bfloat16)


def general_body(
    queries,
    keys,
    values,
    prefix_resid,
    opt_queries,
    opt_keys,
    opt_values,
    opt_resid,
    out_weight,
    norm_gain,
    option_bounds,
):
    local_rows = queries.shape[0]
    opt_len = opt_queries.shape[1]
    seq_count = lax.axis_size("seq")
    seq_index = lax.axis_index("seq")
    halo_count = WINDOW // local_rows
    earlier_keys = []
    earlier_values = []
    carried = (keys, values)
    for hop_index in range(halo_count):
        carried = passed_along((carried[0], carried[1]), "seq", 1)
        earlier_keys.insert(0, carried[0])
        earlier_values.insert(0, carried[1])
    window_keys = jnp.concatenate(earlier_keys + [keys], axis=0)
    window_values = jnp.concatenate(earlier_values + [values], axis=0)
    query_pos = seq_index * local_rows + jnp.arange(local_rows, dtype=jnp.int32)
    key_pos = (seq_index - halo_count) * local_rows + jnp.arange(
        window_keys.shape[0], dtype=jnp.int32
    )
    allowed = (
        (key_pos[None] <= query_pos[:, None])
        & (key_pos[None] > query_pos[:, None] - WINDOW)
        & (key_pos[None] >= 0)
    )
    prefix_attn = attend(queries, window_keys, window_values, allowed)
    final_keys, final_values = (
        from_root(window_keys[local_rows:], "seq", seq_count - 1),
        from_root(window_values[local_rows:], "seq", seq_count - 1),
    )
    joined_keys = jnp.concatenate([final_keys, opt_keys[0]], axis=0)
    joined_values = jnp.concatenate([final_values, opt_values[0]], axis=0)
    positions = jnp.arange(WINDOW + opt_len, dtype=jnp.int32)
    option_pos = jnp.arange(opt_len, dtype=jnp.int32)
    option_allowed = jnp.where(
        positions[None] < WINDOW,
        positions[None] > option_pos[:, None],
        positions[None] - WINDOW <= option_pos[:, None],
    )
    option_attn = attend(opt_queries[0], joined_keys, joined_values, option_allowed)
    stacked = jnp.concatenate([prefix_attn, option_attn], axis=0)
    weight_share = lax.all_gather(out_weight, "seq", axis=0, tiled=True)
    head_cols = stacked.shape[1]
    attn_whole = lax.all_gather(stacked, "head", axis=1, tiled=True)
    projected = jnp.zeros((stacked.shape[0], weight_share.shape[1]), jnp.float32)
    for group in range(lax.axis_size("head")):
        partial_value = jnp.dot(
            attn_whole[:, group * head_cols : (group + 1) * head_cols],
            weight_share[group * head_cols : (group + 1) * head_cols],
            preferred_element_type=jnp.float32,
        )
        projected = projected + lax.optimization_barrier(partial_value.astype(jnp.bfloat16)).astype(
            jnp.float32
        )
    squares = lax.psum(jnp.sum(projected * projected, axis=1), "head")
    width = norm_gain.shape[0] * lax.axis_size("head")
    normed = projected * lax.rsqrt(squares / width + epsilon)[:, None] * norm_gain[None, :]
    prefix_out = (prefix_resid.astype(jnp.float32) + normed[:local_rows]).astype(jnp.bfloat16)
    option_full = opt_resid[0].astype(jnp.float32) + normed[local_rows:]
    start_pos = option_bounds[0, 0]
    length = option_bounds[0, 1]
    inside = option_pos < length
    option_out = jnp.where(inside[:, None], option_full, 0.0).astype(jnp.bfloat16)
    chosen = inside & (option_pos >= start_pos)
    option_summary = jnp.sum(
        jnp.where(chosen[:, None], option_out.astype(jnp.float32), 0.0), axis=0
    ) / (length - start_pos).astype(jnp.float32)
    return (prefix_out, option_out[None], option_summary[None])


SMEM = pltpu.MemorySpace.SMEM
VMEM = pltpu.MemorySpace.VMEM


def dot_nt(a, b):
    return lax.dot_general(a, b, (((1,), (1,)), ((), ())), preferred_element_type=jnp.float32)


def dot_nn(a, b):
    return lax.dot_general(a, b, (((1,), (0,)), ((), ())), preferred_element_type=jnp.float32)


def call(kernel, out_shape, count, flops=0, moved=0, in_specs=None, scratch=()):
    many = isinstance(out_shape, (list, tuple))
    return pl.pallas_call(
        kernel,
        out_shape=out_shape,
        in_specs=in_specs or [pl.BlockSpec(memory_space=VMEM)] * count,
        out_specs=[pl.BlockSpec(memory_space=VMEM)] * len(out_shape)
        if many
        else pl.BlockSpec(memory_space=VMEM),
        scratch_shapes=list(scratch),
        cost_estimate=pl.CostEstimate(flops=flops, bytes_accessed=moved, transcendentals=0),
        compiler_params=pltpu.CompilerParams(vmem_limit_bytes=VMEM_BYTES),
    )


def masks(s):
    parity = lax.rem(s, 2)
    return (0 * parity, 4 - 2 * parity, 2 + 2 * parity, 0 * parity + 6)


def pack_kernel(q, kt, vt, oq, ok, ov, keep_kv, send_kv, keep_q, send_q):
    parity = lax.rem(lax.axis_index("seq"), 2)
    rows, opt = q.shape[0], oq.shape[1]
    wide = q.shape[1] // 2
    for kv, qs, head in ((keep_kv, keep_q, parity), (send_kv, send_q, 1 - parity)):
        at = pl.multiple_of(head * HD, HD)
        at_q = pl.multiple_of(head * wide, wide)
        kv[0:HD, :] = kt[pl.ds(at, HD), :]
        kv[HD : 2 * HD, :] = vt[pl.ds(at, HD), :]
        qs[0:rows, :] = q[:, pl.ds(at_q, wide)]
        qs[rows : rows + opt, :] = oq[0, :, pl.ds(at_q, wide)]
        qs[rows + opt : rows + 2 * opt, 0:HD] = ok[0, :, pl.ds(at, HD)]
        qs[rows + opt : rows + 2 * opt, HD : 2 * HD] = ov[0, :, pl.ds(at, HD)]


def attn_kernel(flip, rows, opt, kv0, kv1, kv2, kv3, qs, out):
    s = lax.axis_index("seq")
    slots = (kv0, kv1, kv2, kv3)
    keys = jnp.concatenate(
        [kv[b * 2 * HD : b * 2 * HD + HD, :] for kv in slots for b in (0, 1)], axis=1
    )
    values = jnp.concatenate(
        [kv[b * 2 * HD + HD : (b + 1) * 2 * HD, :] for kv in slots for b in (0, 1)], axis=1
    )
    lane = lax.broadcasted_iota(jnp.int32, (1, rows), 1)
    key_pos = jnp.concatenate(
        [((s ^ m) ^ b) * rows + lane for m in masks(s) for b in (0, 1)], axis=1
    )
    query_pos = (s ^ flip) * rows + lax.broadcasted_iota(jnp.int32, (rows, 1), 0)
    heads = qs.shape[1] // HD
    for h in range(heads):
        scores = dot_nn(qs[0:rows, h * HD : (h + 1) * HD], keys)
        scores = jnp.where(key_pos <= query_pos, scores, -jnp.inf)
        top = jnp.max(scores, axis=1, keepdims=True)
        weights = jnp.exp2((scores - top) * exp2_scale)
        total = jnp.sum(weights, axis=1, keepdims=True)
        mixed = dot_nt(weights.astype(jnp.bfloat16), values)
        out[0:rows, h * HD : (h + 1) * HD] = (mixed / total).astype(jnp.bfloat16)
    oq = jnp.concatenate([qs[rows : rows + opt, h * HD : (h + 1) * HD] for h in range(heads)], axis=0)
    own_keys = qs[rows + opt : rows + 2 * opt, 0:HD]
    own_values = qs[rows + opt : rows + 2 * opt, HD : 2 * HD]
    step = lax.rem(lax.broadcasted_iota(jnp.int32, (heads * opt, 1), 0), opt)
    scores = jnp.where(key_pos > step, dot_nn(oq, keys), -jnp.inf)
    own = dot_nt(oq, own_keys)
    own = jnp.where(lax.broadcasted_iota(jnp.int32, (1, opt), 1) <= step, own, -jnp.inf)
    top = jnp.maximum(
        jnp.max(scores, axis=1, keepdims=True), jnp.max(own, axis=1, keepdims=True)
    )
    weights = jnp.exp2((scores - top) * exp2_scale)
    own = jnp.exp2((own - top) * exp2_scale)
    total = jnp.sum(weights, axis=1, keepdims=True) + jnp.sum(own, axis=1, keepdims=True)
    mixed = dot_nt(weights.astype(jnp.bfloat16), values) + dot_nn(
        own.astype(jnp.bfloat16), own_values
    )
    mixed = (mixed / total).astype(jnp.bfloat16)
    for h in range(heads):
        out[rows : rows + opt, h * HD : (h + 1) * HD] = mixed[h * opt : (h + 1) * opt]


def project_kernel(w0, w1, w2, w3, a0, a1, a2, a3, out, held, placed, sems):
    copies = [
        pltpu.make_async_copy(w, held.at[j], sems.at[j]) for j, w in enumerate((w0, w1, w2, w3))
    ]
    for copy in copies:
        copy.start()
    s = lax.axis_index("seq")
    z = lax.axis_index("head")
    place = z ^ (z >> 1)
    for t, a in enumerate((a0, a1, a2, a3)):
        source = lax.rem(place + (4 - t), 4)
        placed[source ^ (source >> 1)] = a[...]
    for copy in copies:
        copy.wait()
    blocks = [placed[(s ^ m) >> 1] for m in masks(s)]
    features = out.shape[0]
    part = features // 3
    for n in range(3):
        total = dot_nt(held[0, n * part : (n + 1) * part, :], blocks[0])
        for j in range(1, 4):
            total += dot_nt(held[j, n * part : (n + 1) * part, :], blocks[j])
        out[n * part : (n + 1) * part, :] = total.astype(out.dtype)


def square_kernel(own, received, projected, squares):
    total = own[...] + received[...].astype(jnp.float32)
    projected[...] = total
    squares[...] = jnp.sum(total * total, axis=0, keepdims=True)


def spread_kernel(gain, out):
    out[...] = jnp.broadcast_to(gain[...], (out.shape[1], out.shape[0])).T


def finish_kernel(
    rows, width, bounds, projected, s0, s1, s2, s3, resid_t, opt_resid, gain, out_t, opt_out, summary
):
    squares = s0[...] + s1[...] + s2[...] + s3[...]
    scale = lax.rsqrt(squares / width + epsilon)
    spread = gain[...]
    normed = projected[:, 0:rows] * scale[:, 0:rows] * spread
    out_t[...] = (resid_t[...].astype(jnp.float32) + normed).astype(jnp.bfloat16)
    opt = opt_resid.shape[1]
    normed = projected[:, rows : rows + opt] * scale[:, rows : rows + opt] * spread[:, 0:opt]
    full = opt_resid[0].astype(jnp.float32) + normed.T
    start, length = bounds[0, 0], bounds[0, 1]
    position = lax.broadcasted_iota(jnp.int32, (opt, 1), 0)
    kept = jnp.where(position < length, full, 0.0).astype(jnp.bfloat16)
    opt_out[0] = kept
    chosen = (position < length) & (position >= start)
    count = (length - start).astype(jnp.float32)
    summary[...] = (
        jnp.sum(jnp.where(chosen, kept.astype(jnp.float32), 0.0), axis=0, keepdims=True) / count
    )


def paired_body(
    queries,
    keys,
    values,
    prefix_resid,
    opt_queries,
    opt_keys,
    opt_values,
    opt_resid,
    out_weight,
    norm_gain,
    option_bounds,
):
    rows, opt = queries.shape[0], opt_queries.shape[1]
    features = out_weight.shape[1]
    wide = queries.shape[1] // 2
    seq = range(lax.axis_size("seq"))
    bf16, f32 = jnp.bfloat16, jnp.float32
    shape = jax.ShapeDtypeStruct
    pair = [(s, s ^ 1) for s in seq]
    first = [(s, s ^ (2 if s % 2 else 4)) for s in seq]
    second = [(s, s ^ (4 if s % 2 else 2)) for s in seq]
    ring = [(0, 1), (1, 3), (3, 2), (2, 0)]

    def turned(value, steps):
        count = lax.axis_size("head")
        return lax.ppermute(value, "head", [(i, (i + steps) % count) for i in range(count)])

    weight = out_weight.T
    weight_1 = lax.ppermute(weight, "seq", first)

    keep_kv, send_kv, keep_q, send_q = call(
        pack_kernel,
        [shape((2 * HD, rows), bf16)] * 2 + [shape((rows + 2 * opt, wide), bf16)] * 2,
        6,
    )(queries, keys.T, values.T, opt_queries, opt_keys, opt_values)
    pair_kv = lax.ppermute(send_kv, "seq", pair)
    kv_0 = jnp.concatenate([keep_kv, pair_kv], axis=0)
    kv_1 = lax.ppermute(kv_0, "seq", first)
    kv_2 = lax.ppermute(kv_0, "seq", second)
    pair_q = lax.ppermute(send_q, "seq", pair)
    kv_3 = lax.ppermute(kv_1, "seq", second)

    weight_2 = lax.ppermute(weight, "seq", second)
    weight_3 = lax.ppermute(weight_1, "seq", second)
    weights = (weight, weight_1, weight_2, weight_3)

    def attention(flip, q):
        return call(
            functools.partial(attn_kernel, flip, rows, opt),
            shape((rows + opt, wide), bf16),
            5,
            flops=4 * (rows + opt) * wide * WINDOW,
        )(kv_0, kv_1, kv_2, kv_3, q)

    def gathered(block):
        blocks = [block]
        for _ in range(3):
            blocks.append(lax.ppermute(blocks[-1], "head", ring))
        return blocks

    def project(blocks, dtype):
        return call(
            project_kernel,
            shape((features, rows + opt), dtype),
            8,
            flops=8 * features * wide * (rows + opt),
            moved=8 * features * wide,
            in_specs=[pl.BlockSpec(memory_space=pl.ANY)] * 4
            + [pl.BlockSpec(memory_space=VMEM)] * 4,
            scratch=[
                pltpu.VMEM((4, features, wide), bf16),
                pltpu.VMEM((4, rows + opt, wide), bf16),
                pltpu.SemaphoreType.DMA((4,)),
            ],
        )(*weights, *blocks)

    pair_blocks = gathered(attention(1, pair_q))
    own_blocks = gathered(attention(0, keep_q))
    received = lax.ppermute(project(pair_blocks, bf16), "seq", pair)
    own = project(own_blocks, f32)
    projected, squares = call(
        square_kernel, [shape((features, rows + opt), f32), shape((1, rows + opt), f32)], 2
    )(own, received)
    spread = call(spread_kernel, shape((features, rows), f32), 1)(norm_gain[None])
    out_t, opt_out, summary = call(
        functools.partial(finish_kernel, rows, float(features * lax.axis_size("head"))),
        [
            shape((features, rows), bf16),
            shape((1, opt, features), bf16),
            shape((1, features), f32),
        ],
        9,
        in_specs=[pl.BlockSpec(memory_space=SMEM)] + [pl.BlockSpec(memory_space=VMEM)] * 8,
    )(
        option_bounds,
        projected,
        squares,
        turned(squares, 1),
        turned(squares, 2),
        turned(squares, 3),
        prefix_resid.T,
        opt_resid,
        spread,
    )
    return out_t.T, opt_out, summary


def body(*args):
    queries, keys, out_weight = args[0], args[1], args[8]
    seq, head = lax.axis_size("seq"), lax.axis_size("head")
    paired = (
        seq == 8
        and head == 4
        and seq * queries.shape[0] == WINDOW
        and queries.shape[0] == HD
        and keys.shape[1] == 2 * HD
        and out_weight.shape[0] * 2 == queries.shape[1]
        and out_weight.shape[0] * seq == queries.shape[1] * head
    )
    return paired_body(*args) if paired else general_body(*args)


def solution(mesh):
    return jax.shard_map(
        body,
        mesh=mesh,
        in_specs=(
            P("seq", "head"),
            P("seq", "head"),
            P("seq", "head"),
            P("seq", "head"),
            P("seq", None, "head"),
            P("seq", None, "head"),
            P("seq", None, "head"),
            P("seq", None, "head"),
            P("seq", "head"),
            P("head"),
            P("seq", None),
        ),
        out_specs=(P("seq", "head"), P("seq", None, "head"), P("seq", "head")),
        check_vma=False,
    )
```

```python
import functools

import jax
import jax.numpy as jnp
from jax import lax
from jax.experimental import pallas as pl
from jax.experimental.pallas import tpu as pltpu
from jax.sharding import PartitionSpec as P

HD = 128
WINDOW = 1024
score_scale = 168.0 ** (-0.5)
exp2_scale = score_scale * 1.4426950408889634
epsilon = 1e-06


def passed_along(value, axis, steps):
    count = lax.axis_size(axis)
    initial, last = (max(0, -steps), min(count, count - steps))
    return lax.ppermute(value, axis, [(source, source + steps) for source in range(initial, last)])


def from_root(block, axis, owner):
    block = jnp.where(lax.axis_index(axis) == owner, block, jnp.zeros_like(block))
    return lax.psum(block, axis)


def attend(query_rows, key_rows, value_rows, allowed):
    row_count = query_rows.shape[0]
    kv_heads = key_rows.shape[1] // HD
    groups = query_rows.shape[1] // key_rows.shape[1]
    query_view = query_rows.reshape(row_count, kv_heads, groups, HD)
    key_view = key_rows.reshape(-1, kv_heads, HD)
    scores = (
        jnp.einsum("rkgd,lkd->kgrl", query_view, key_view, preferred_element_type=jnp.float32)
        * score_scale
    )
    scores = jnp.where(allowed[None, None], scores, -jnp.inf)
    row_max = jnp.max(scores, axis=-1, keepdims=True)
    weights = jnp.exp(scores - row_max)
    weights = (weights / jnp.sum(weights, axis=-1, keepdims=True)).astype(jnp.bfloat16)
    value_view = value_rows.reshape(-1, kv_heads, HD)
    attended = jnp.einsum("kgrl,lkd->rkgd", weights, value_view, preferred_element_type=jnp.float32)
    return attended.reshape(row_count, -1).astype(jnp.bfloat16)


def general_body(
    queries,
    keys,
    values,
    prefix_resid,
    opt_queries,
    opt_keys,
    opt_values,
    opt_resid,
    out_weight,
    norm_gain,
    option_bounds,
):
    local_rows = queries.shape[0]
    opt_len = opt_queries.shape[1]
    seq_count = lax.axis_size("seq")
    seq_index = lax.axis_index("seq")
    halo_count = WINDOW // local_rows
    earlier_keys = []
    earlier_values = []
    carried = (keys, values)
    for hop_index in range(halo_count):
        carried = passed_along((carried[0], carried[1]), "seq", 1)
        earlier_keys.insert(0, carried[0])
        earlier_values.insert(0, carried[1])
    window_keys = jnp.concatenate(earlier_keys + [keys], axis=0)
    window_values = jnp.concatenate(earlier_values + [values], axis=0)
    query_pos = seq_index * local_rows + jnp.arange(local_rows, dtype=jnp.int32)
    key_pos = (seq_index - halo_count) * local_rows + jnp.arange(
        window_keys.shape[0], dtype=jnp.int32
    )
    allowed = (
        (key_pos[None] <= query_pos[:, None])
        & (key_pos[None] > query_pos[:, None] - WINDOW)
        & (key_pos[None] >= 0)
    )
    prefix_attn = attend(queries, window_keys, window_values, allowed)
    final_keys, final_values = (
        from_root(window_keys[local_rows:], "seq", seq_count - 1),
        from_root(window_values[local_rows:], "seq", seq_count - 1),
    )
    joined_keys = jnp.concatenate([final_keys, opt_keys[0]], axis=0)
    joined_values = jnp.concatenate([final_values, opt_values[0]], axis=0)
    positions = jnp.arange(WINDOW + opt_len, dtype=jnp.int32)
    option_pos = jnp.arange(opt_len, dtype=jnp.int32)
    option_allowed = jnp.where(
        positions[None] < WINDOW,
        positions[None] > option_pos[:, None],
        positions[None] - WINDOW <= option_pos[:, None],
    )
    option_attn = attend(opt_queries[0], joined_keys, joined_values, option_allowed)
    stacked = jnp.concatenate([prefix_attn, option_attn], axis=0)
    weight_share = lax.all_gather(out_weight, "seq", axis=0, tiled=True)
    head_cols = stacked.shape[1]
    attn_whole = lax.all_gather(stacked, "head", axis=1, tiled=True)
    projected = jnp.zeros((stacked.shape[0], weight_share.shape[1]), jnp.float32)
    for group in range(lax.axis_size("head")):
        partial_value = jnp.dot(
            attn_whole[:, group * head_cols : (group + 1) * head_cols],
            weight_share[group * head_cols : (group + 1) * head_cols],
            preferred_element_type=jnp.float32,
        )
        projected = projected + lax.optimization_barrier(partial_value.astype(jnp.bfloat16)).astype(
            jnp.float32
        )
    squares = lax.psum(jnp.sum(projected * projected, axis=1), "head")
    width = norm_gain.shape[0] * lax.axis_size("head")
    normed = projected * lax.rsqrt(squares / width + epsilon)[:, None] * norm_gain[None, :]
    prefix_out = (prefix_resid.astype(jnp.float32) + normed[:local_rows]).astype(jnp.bfloat16)
    option_full = opt_resid[0].astype(jnp.float32) + normed[local_rows:]
    start_pos = option_bounds[0, 0]
    length = option_bounds[0, 1]
    inside = option_pos < length
    option_out = jnp.where(inside[:, None], option_full, 0.0).astype(jnp.bfloat16)
    chosen = inside & (option_pos >= start_pos)
    option_summary = jnp.sum(
        jnp.where(chosen[:, None], option_out.astype(jnp.float32), 0.0), axis=0
    ) / (length - start_pos).astype(jnp.float32)
    return (prefix_out, option_out[None], option_summary[None])


SMEM = pltpu.MemorySpace.SMEM
VMEM = pltpu.MemorySpace.VMEM
HBM = pltpu.MemorySpace.HBM


def dot_nt(a, b):
    return lax.dot_general(a, b, (((1,), (1,)), ((), ())), preferred_element_type=jnp.float32)


def dot_nn(a, b):
    return lax.dot_general(a, b, (((1,), (0,)), ((), ())), preferred_element_type=jnp.float32)


def call(kernel, out_shape, count, flops=0, moved=0, in_specs=None, out_specs=None, scratch=(), vmem=8):
    many = isinstance(out_shape, (list, tuple))
    return pl.pallas_call(
        kernel,
        out_shape=out_shape,
        in_specs=in_specs or [pl.BlockSpec(memory_space=VMEM)] * count,
        out_specs=out_specs
        or ([pl.BlockSpec(memory_space=VMEM)] * len(out_shape) if many else pl.BlockSpec(memory_space=VMEM)),
        scratch_shapes=list(scratch),
        cost_estimate=pl.CostEstimate(flops=flops, bytes_accessed=moved, transcendentals=0),
        compiler_params=pltpu.CompilerParams(vmem_limit_bytes=vmem * 1024 * 1024),
    )


def masks(s):
    parity = lax.rem(s, 2)
    return (0 * parity, 4 - 2 * parity, 2 + 2 * parity, 0 * parity + 6)


def pack_kernel(q, k, v, oq, ok, ov, sent, kept, sems):
    parity = lax.rem(lax.axis_index("seq"), 2)
    rows, opt = q.shape[0], oq.shape[1]
    wide = q.shape[1] // 2
    own = pl.ds(2 * rows + opt, opt)
    pieces = []
    for to, head in ((sent, 1 - parity), (kept, parity)):
        at = pl.ds(pl.multiple_of(head * HD, HD), HD)
        at_q = pl.ds(pl.multiple_of(head * wide, wide), wide)
        pieces += [
            (k.at[:, at], to.at[0:rows, 0:HD]),
            (v.at[:, at], to.at[0:rows, HD : 2 * HD]),
            (q.at[:, at_q], to.at[rows : 2 * rows, :]),
            (oq.at[0, :, at_q], to.at[2 * rows : 2 * rows + opt, :]),
            (ok.at[0, :, at], to.at[own, 0:HD]),
            (ov.at[0, :, at], to.at[own, HD : 2 * HD]),
        ]
    copies = [pltpu.make_async_copy(a, b, sems.at[i]) for i, (a, b) in enumerate(pieces)]
    for copy in copies:
        copy.start()
    for copy in copies:
        copy.wait()


def join_kernel(kept, received, out):
    rows = out.shape[0] // 2
    out[0:rows, :] = kept[0:rows, :]
    out[rows : 2 * rows, :] = received[0:rows, :]


def stack_kernel(upper, lower, out):
    rows = upper.shape[0]
    out[0:rows, :] = upper[...]
    out[rows : 2 * rows, :] = lower[...]


def attn_kernel(flip, rows, opt, kv02, kv13, packed, out):
    own = slice(2 * rows + opt, 2 * rows + 2 * opt)
    attn(
        (kv02, kv13),
        flip,
        packed[rows : 2 * rows, :],
        packed[2 * rows : 2 * rows + opt, :],
        packed[own, 0:HD],
        packed[own, HD : 2 * HD],
        out,
    )


def attn(slots, flip, q, oq, own_keys, own_values, out):
    s = lax.axis_index("seq")
    rows, opt = q.shape[0], oq.shape[0]
    keys = jnp.concatenate([kv[:, 0:HD] for kv in slots], axis=0)
    values = jnp.concatenate([kv[:, HD : 2 * HD] for kv in slots], axis=0)
    _, m1, m2, m3 = masks(s)
    lane = lax.broadcasted_iota(jnp.int32, (1, rows), 1)
    key_pos = jnp.concatenate(
        [((s ^ m) ^ b) * rows + lane for m in (0, m2, m1, m3) for b in (0, 1)], axis=1
    )
    query_pos = (s ^ flip) * rows + lax.broadcasted_iota(jnp.int32, (rows, 1), 0)
    heads = q.shape[1] // HD
    for h in range(heads):
        scores = dot_nt(q[:, h * HD : (h + 1) * HD], keys)
        scores = jnp.where(key_pos <= query_pos, scores, -jnp.inf)
        top = jnp.max(scores, axis=1, keepdims=True)
        weights = jnp.exp2((scores - top) * exp2_scale)
        total = jnp.sum(weights, axis=1, keepdims=True)
        mixed = dot_nn(weights.astype(jnp.bfloat16), values)
        out[0:rows, h * HD : (h + 1) * HD] = (mixed / total).astype(jnp.bfloat16)
    oq = jnp.concatenate([oq[:, h * HD : (h + 1) * HD] for h in range(heads)], axis=0)
    step = lax.rem(lax.broadcasted_iota(jnp.int32, (heads * opt, 1), 0), opt)
    scores = jnp.where(key_pos > step, dot_nt(oq, keys), -jnp.inf)
    own = dot_nt(oq, own_keys)
    own = jnp.where(lax.broadcasted_iota(jnp.int32, (1, opt), 1) <= step, own, -jnp.inf)
    top = jnp.maximum(
        jnp.max(scores, axis=1, keepdims=True), jnp.max(own, axis=1, keepdims=True)
    )
    weights = jnp.exp2((scores - top) * exp2_scale)
    own = jnp.exp2((own - top) * exp2_scale)
    total = jnp.sum(weights, axis=1, keepdims=True) + jnp.sum(own, axis=1, keepdims=True)
    mixed = dot_nn(weights.astype(jnp.bfloat16), values) + dot_nn(
        own.astype(jnp.bfloat16), own_values
    )
    mixed = (mixed / total).astype(jnp.bfloat16)
    for h in range(heads):
        out[rows : rows + opt, h * HD : (h + 1) * HD] = mixed[h * opt : (h + 1) * opt]


def project_kernel(rows, opt, packed, w0, w1, w2, w3, a0, a1, a2, a3, out, placed):
    s = lax.axis_index("seq")
    z = lax.axis_index("head")
    for t, a in enumerate((a0, a1, a2, a3)):
        placed[z ^ t] = a[...]
    blocks = [placed[(s ^ m) >> 1] for m in masks(s)]
    held = (w0, w1, w2, w3)
    features = w0.shape[0]
    half = features // 2
    for n in range(2):
        part = slice(n * half, (n + 1) * half)
        total = dot_nt(held[0][part, :], blocks[0])
        for j in range(1, 4):
            total += dot_nt(held[j][part, :], blocks[j])
        total = total.astype(out.dtype)
        if packed:
            out[part, :] = total[:, 0:rows]
            out[features : features + half, n * opt : (n + 1) * opt] = total[:, rows : rows + opt]
        else:
            out[part, :] = total


def square_kernel(rows, opt, own, received, projected, squares):
    features = own.shape[0]
    half = features // 2
    left = own[:, 0:rows] + received[0:features, :].astype(jnp.float32)
    projected[:, 0:rows] = left
    squares[:, 0:rows] = jnp.sum(left * left, axis=0, keepdims=True)
    total = 0.0
    for n in range(2):
        part = slice(n * half, (n + 1) * half)
        right = received[features : features + half, n * opt : (n + 1) * opt]
        right = own[part, rows : rows + opt] + right.astype(jnp.float32)
        projected[part, rows : rows + opt] = right
        total += jnp.sum(right * right, axis=0, keepdims=True)
    squares[:, rows : rows + opt] = total


def scale_kernel(rows, projected, gain, prefix, option):
    features = prefix.shape[0]
    row = gain[...]
    prefix[...] = projected[:, 0:rows] * jnp.broadcast_to(row, (rows, features)).T
    option[...] = projected[:, rows:].T * row


def finish_kernel(
    rows, width, bounds, prefix, option, s0, s1, s2, s3, resid_t, opt_resid,
    out_t, opt_out, summary, held_t, held_opt, held_sum, sems,
):
    squares = s0[...] + s1[...] + s2[...] + s3[...]
    scale = lax.rsqrt(squares / width + epsilon)
    held_t[...] = (resid_t[...].astype(jnp.float32) + prefix[...] * scale[:, 0:rows]).astype(
        jnp.bfloat16
    )
    copies = [
        pltpu.make_async_copy(a, b, sems.at[i])
        for i, (a, b) in enumerate(((held_t, out_t), (held_opt, opt_out), (held_sum, summary)))
    ]
    copies[0].start()
    opt = opt_resid.shape[1]
    column = jnp.broadcast_to(scale[:, rows : rows + opt], (HD, opt)).T[:, 0:1]
    full = opt_resid[0].astype(jnp.float32) + option[...] * column
    start, length = bounds[0, 0], bounds[0, 1]
    position = lax.broadcasted_iota(jnp.int32, (opt, 1), 0)
    kept = jnp.where(position < length, full, 0.0).astype(jnp.bfloat16)
    held_opt[0] = kept
    copies[1].start()
    chosen = (position < length) & (position >= start)
    count = (length - start).astype(jnp.float32)
    held_sum[...] = (
        jnp.sum(jnp.where(chosen, kept.astype(jnp.float32), 0.0), axis=0, keepdims=True) / count
    )
    copies[2].start()
    for copy in copies:
        copy.wait()


def paired_body(
    queries,
    keys,
    values,
    prefix_resid,
    opt_queries,
    opt_keys,
    opt_values,
    opt_resid,
    out_weight,
    norm_gain,
    option_bounds,
):
    rows, opt = queries.shape[0], opt_queries.shape[1]
    features = out_weight.shape[1]
    wide = queries.shape[1] // 2
    seq = range(lax.axis_size("seq"))
    bf16, f32 = jnp.bfloat16, jnp.float32
    shape = jax.ShapeDtypeStruct
    pair = [(s, s ^ 1) for s in seq]
    first = [(s, s ^ (2 if s % 2 else 4)) for s in seq]
    second = [(s, s ^ (4 if s % 2 else 2)) for s in seq]

    def turned(value, steps):
        count = lax.axis_size("head")
        return lax.ppermute(value, "head", [(i, (i + steps) % count) for i in range(count)])

    def after(value, *others):
        return lax.optimization_barrier((value, *others))[0]

    def in_hbm(value):
        return pltpu.with_memory_space_constraint(value, HBM)

    def crossed(value, mask):
        return lax.ppermute(value, "head", [(i, i ^ mask) for i in range(lax.axis_size("head"))])

    weight = out_weight.T
    weight_1 = lax.ppermute(weight, "seq", first)

    packed = pltpu.VMEM((2 * rows + 2 * opt, wide), bf16)
    sent, kept = call(
        pack_kernel,
        [packed, packed],
        6,
        in_specs=[pl.BlockSpec(memory_space=HBM)] * 6,
        scratch=[pltpu.SemaphoreType.DMA((12,))],
    )(*map(in_hbm, (queries, keys, values, opt_queries, opt_keys, opt_values)))
    received = lax.ppermute(sent, "seq", pair)
    kv_0 = call(join_kernel, pltpu.VMEM((2 * rows, 2 * HD), bf16), 2)(kept, received)
    kv_2 = lax.ppermute(kv_0, "seq", second)
    kv_02 = call(stack_kernel, pltpu.VMEM((4 * rows, 2 * HD), bf16), 2)(kv_0, kv_2)
    kv_13 = lax.ppermute(kv_02, "seq", first)

    attn_shape = pltpu.VMEM((rows + opt, wide), bf16)

    def attention(flip, block):
        return call(
            functools.partial(attn_kernel, flip, rows, opt),
            attn_shape,
            3,
            flops=4 * (rows + opt) * wide * WINDOW,
            vmem=24,
        )(kv_02, kv_13, block)

    pair_0 = attention(1, received)
    own_0 = attention(0, kept)
    pair_1, pair_2 = crossed(pair_0, 1), crossed(pair_0, 2)
    own_1, own_2 = crossed(own_0, 1), crossed(own_0, 2)
    pair_3 = crossed(after(pair_2, own_0), 1)
    own_3 = crossed(own_2, 1)

    weight_2 = lax.ppermute(after(weight, kv_13), "seq", second)
    weight_3 = lax.ppermute(after(weight_1, kv_13), "seq", second)
    weights = (weight, weight_1, weight_2, weight_3)

    def project(blocks, out_shape, packed):
        return call(
            functools.partial(project_kernel, rows, opt, packed),
            out_shape,
            8,
            flops=8 * features * wide * (rows + opt),
            moved=8 * features * wide,
            scratch=[pltpu.VMEM((4, rows + opt, wide), bf16)],
            vmem=16,
        )(*weights, *blocks)

    half = project((after(pair_0, own_1, own_3), pair_1, pair_2, pair_3), shape((features + features // 2, rows), bf16), True)
    received = lax.ppermute(half, "seq", pair)
    own = project((own_0, own_1, own_2, own_3), shape((features, rows + opt), f32), False)
    projected, squares = call(
        functools.partial(square_kernel, rows, opt),
        [shape((features, rows + opt), f32), shape((1, rows + opt), f32)],
        2,
    )(own, received)
    prefix, option = call(
        functools.partial(scale_kernel, rows),
        [shape((features, rows), f32), shape((opt, features), f32)],
        2,
    )(projected, norm_gain[None])
    results = [
        shape((features, rows), bf16),
        shape((1, opt, features), bf16),
        shape((1, features), f32),
    ]
    out_t, opt_out, summary = call(
        functools.partial(finish_kernel, rows, float(features * lax.axis_size("head"))),
        results,
        9,
        in_specs=[pl.BlockSpec(memory_space=SMEM)] + [pl.BlockSpec(memory_space=VMEM)] * 8,
        out_specs=[pl.BlockSpec(memory_space=HBM)] * 3,
        scratch=[pltpu.VMEM(r.shape, r.dtype) for r in results] + [pltpu.SemaphoreType.DMA((3,))],
    )(
        option_bounds,
        prefix,
        option,
        squares,
        turned(squares, 1),
        turned(squares, 2),
        turned(squares, 3),
        prefix_resid.T,
        opt_resid,
    )
    return out_t.T, opt_out, summary


def body(*args):
    queries, keys, opt_queries, out_weight = args[0], args[1], args[4], args[8]
    seq, head = lax.axis_size("seq"), lax.axis_size("head")
    paired = (
        seq == 8
        and head == 4
        and seq * queries.shape[0] == WINDOW
        and queries.shape[0] == HD
        and queries.shape[0] == 2 * opt_queries.shape[1]
        and keys.shape[1] == 2 * HD
        and out_weight.shape[0] * 2 == queries.shape[1]
        and out_weight.shape[0] * seq == queries.shape[1] * head
    )
    return paired_body(*args) if paired else general_body(*args)


def solution(mesh):
    return jax.shard_map(
        body,
        mesh=mesh,
        in_specs=(
            P("seq", "head"),
            P("seq", "head"),
            P("seq", "head"),
            P("seq", "head"),
            P("seq", None, "head"),
            P("seq", None, "head"),
            P("seq", None, "head"),
            P("seq", None, "head"),
            P("seq", "head"),
            P("head"),
            P("seq", None),
        ),
        out_specs=(P("seq", "head"), P("seq", None, "head"), P("seq", "head")),
        check_vma=False,
    )
```

```python
import functools

import jax
import jax.numpy as jnp
from jax import lax
from jax.experimental import pallas as pl
from jax.experimental.pallas import tpu as pltpu
from jax.sharding import PartitionSpec as P

HD = 128
WINDOW = 1024
score_scale = 168.0 ** (-0.5)
exp2_scale = score_scale * 1.4426950408889634
epsilon = 1e-06


def passed_along(value, axis, steps):
    count = lax.axis_size(axis)
    initial, last = (max(0, -steps), min(count, count - steps))
    return lax.ppermute(value, axis, [(source, source + steps) for source in range(initial, last)])


def from_root(block, axis, owner):
    block = jnp.where(lax.axis_index(axis) == owner, block, jnp.zeros_like(block))
    return lax.psum(block, axis)


def attend(query_rows, key_rows, value_rows, allowed):
    row_count = query_rows.shape[0]
    kv_heads = key_rows.shape[1] // HD
    groups = query_rows.shape[1] // key_rows.shape[1]
    query_view = query_rows.reshape(row_count, kv_heads, groups, HD)
    key_view = key_rows.reshape(-1, kv_heads, HD)
    scores = (
        jnp.einsum("rkgd,lkd->kgrl", query_view, key_view, preferred_element_type=jnp.float32)
        * score_scale
    )
    scores = jnp.where(allowed[None, None], scores, -jnp.inf)
    row_max = jnp.max(scores, axis=-1, keepdims=True)
    weights = jnp.exp(scores - row_max)
    weights = (weights / jnp.sum(weights, axis=-1, keepdims=True)).astype(jnp.bfloat16)
    value_view = value_rows.reshape(-1, kv_heads, HD)
    attended = jnp.einsum("kgrl,lkd->rkgd", weights, value_view, preferred_element_type=jnp.float32)
    return attended.reshape(row_count, -1).astype(jnp.bfloat16)


def general_body(
    queries,
    keys,
    values,
    prefix_resid,
    opt_queries,
    opt_keys,
    opt_values,
    opt_resid,
    out_weight,
    norm_gain,
    option_bounds,
):
    local_rows = queries.shape[0]
    opt_len = opt_queries.shape[1]
    seq_count = lax.axis_size("seq")
    seq_index = lax.axis_index("seq")
    halo_count = WINDOW // local_rows
    earlier_keys = []
    earlier_values = []
    carried = (keys, values)
    for hop_index in range(halo_count):
        carried = passed_along((carried[0], carried[1]), "seq", 1)
        earlier_keys.insert(0, carried[0])
        earlier_values.insert(0, carried[1])
    window_keys = jnp.concatenate(earlier_keys + [keys], axis=0)
    window_values = jnp.concatenate(earlier_values + [values], axis=0)
    query_pos = seq_index * local_rows + jnp.arange(local_rows, dtype=jnp.int32)
    key_pos = (seq_index - halo_count) * local_rows + jnp.arange(
        window_keys.shape[0], dtype=jnp.int32
    )
    allowed = (
        (key_pos[None] <= query_pos[:, None])
        & (key_pos[None] > query_pos[:, None] - WINDOW)
        & (key_pos[None] >= 0)
    )
    prefix_attn = attend(queries, window_keys, window_values, allowed)
    final_keys, final_values = (
        from_root(window_keys[local_rows:], "seq", seq_count - 1),
        from_root(window_values[local_rows:], "seq", seq_count - 1),
    )
    joined_keys = jnp.concatenate([final_keys, opt_keys[0]], axis=0)
    joined_values = jnp.concatenate([final_values, opt_values[0]], axis=0)
    positions = jnp.arange(WINDOW + opt_len, dtype=jnp.int32)
    option_pos = jnp.arange(opt_len, dtype=jnp.int32)
    option_allowed = jnp.where(
        positions[None] < WINDOW,
        positions[None] > option_pos[:, None],
        positions[None] - WINDOW <= option_pos[:, None],
    )
    option_attn = attend(opt_queries[0], joined_keys, joined_values, option_allowed)
    stacked = jnp.concatenate([prefix_attn, option_attn], axis=0)
    weight_share = lax.all_gather(out_weight, "seq", axis=0, tiled=True)
    head_cols = stacked.shape[1]
    attn_whole = lax.all_gather(stacked, "head", axis=1, tiled=True)
    projected = jnp.zeros((stacked.shape[0], weight_share.shape[1]), jnp.float32)
    for group in range(lax.axis_size("head")):
        partial_value = jnp.dot(
            attn_whole[:, group * head_cols : (group + 1) * head_cols],
            weight_share[group * head_cols : (group + 1) * head_cols],
            preferred_element_type=jnp.float32,
        )
        projected = projected + lax.optimization_barrier(partial_value.astype(jnp.bfloat16)).astype(
            jnp.float32
        )
    squares = lax.psum(jnp.sum(projected * projected, axis=1), "head")
    width = norm_gain.shape[0] * lax.axis_size("head")
    normed = projected * lax.rsqrt(squares / width + epsilon)[:, None] * norm_gain[None, :]
    prefix_out = (prefix_resid.astype(jnp.float32) + normed[:local_rows]).astype(jnp.bfloat16)
    option_full = opt_resid[0].astype(jnp.float32) + normed[local_rows:]
    start_pos = option_bounds[0, 0]
    length = option_bounds[0, 1]
    inside = option_pos < length
    option_out = jnp.where(inside[:, None], option_full, 0.0).astype(jnp.bfloat16)
    chosen = inside & (option_pos >= start_pos)
    option_summary = jnp.sum(
        jnp.where(chosen[:, None], option_out.astype(jnp.float32), 0.0), axis=0
    ) / (length - start_pos).astype(jnp.float32)
    return (prefix_out, option_out[None], option_summary[None])


LONG_P, LONG_O, LONG_M = 200, 1, 14


SMEM = pltpu.MemorySpace.SMEM
VMEM = pltpu.MemorySpace.VMEM
HBM = pltpu.MemorySpace.HBM


def dot_nt(a, b):
    return lax.dot_general(a, b, (((1,), (1,)), ((), ())), preferred_element_type=jnp.float32)


def dot_nn(a, b):
    return lax.dot_general(a, b, (((1,), (0,)), ((), ())), preferred_element_type=jnp.float32)


def call(kernel, out_shape, count, flops=0, moved=0, in_specs=None, out_specs=None, scratch=(), vmem=8):
    many = isinstance(out_shape, (list, tuple))
    return pl.pallas_call(
        kernel,
        out_shape=out_shape,
        in_specs=in_specs or [pl.BlockSpec(memory_space=VMEM)] * count,
        out_specs=out_specs
        or ([pl.BlockSpec(memory_space=VMEM)] * len(out_shape) if many else pl.BlockSpec(memory_space=VMEM)),
        scratch_shapes=list(scratch),
        cost_estimate=pl.CostEstimate(flops=flops, bytes_accessed=moved, transcendentals=0),
        compiler_params=pltpu.CompilerParams(vmem_limit_bytes=vmem * 1024 * 1024),
    )


def masks(s):
    parity = lax.rem(s, 2)
    return (0 * parity, 4 - 2 * parity, 2 + 2 * parity, 0 * parity + 6)


def pack_kernel(q, k, v, oq, ok, ov, sent, kept, sems):
    parity = lax.rem(lax.axis_index("seq"), 2)
    rows, opt = q.shape[0], oq.shape[1]
    wide = q.shape[1] // 2
    own = pl.ds(2 * rows + opt, opt)
    pieces = []
    for to, head in ((sent, 1 - parity), (kept, parity)):
        at = pl.ds(pl.multiple_of(head * HD, HD), HD)
        at_q = pl.ds(pl.multiple_of(head * wide, wide), wide)
        pieces += [
            (k.at[:, at], to.at[0:rows, 0:HD]),
            (v.at[:, at], to.at[0:rows, HD : 2 * HD]),
            (q.at[:, at_q], to.at[rows : 2 * rows, :]),
            (oq.at[0, :, at_q], to.at[2 * rows : 2 * rows + opt, :]),
            (ok.at[0, :, at], to.at[own, 0:HD]),
            (ov.at[0, :, at], to.at[own, HD : 2 * HD]),
        ]
    copies = [pltpu.make_async_copy(a, b, sems.at[i]) for i, (a, b) in enumerate(pieces)]
    for copy in copies:
        copy.start()
    for copy in copies:
        copy.wait()


def join_kernel(kept, received, out):
    rows = out.shape[0] // 2
    out[0:rows, :] = kept[0:rows, :]
    out[rows : 2 * rows, :] = received[0:rows, :]


def attn_kernel(flip, rows, opt, kv0, kv1, kv2, kv3, packed, out):
    own = slice(2 * rows + opt, 2 * rows + 2 * opt)
    attn(
        (kv0, kv1, kv2, kv3),
        flip,
        packed[rows : 2 * rows, :],
        packed[2 * rows : 2 * rows + opt, :],
        packed[own, 0:HD],
        packed[own, HD : 2 * HD],
        out,
    )


def attn(slots, flip, q, oq, own_keys, own_values, out):
    s = lax.axis_index("seq")
    rows, opt = q.shape[0], oq.shape[0]
    keys = jnp.concatenate([kv[:, 0:HD] for kv in slots], axis=0)
    values = jnp.concatenate([kv[:, HD : 2 * HD] for kv in slots], axis=0)
    lane = lax.broadcasted_iota(jnp.int32, (1, rows), 1)
    key_pos = jnp.concatenate(
        [((s ^ m) ^ b) * rows + lane for m in masks(s) for b in (0, 1)], axis=1
    )
    query_pos = (s ^ flip) * rows + lax.broadcasted_iota(jnp.int32, (rows, 1), 0)
    heads = q.shape[1] // HD
    for h in range(heads):
        scores = dot_nt(q[:, h * HD : (h + 1) * HD], keys)
        scores = jnp.where(key_pos <= query_pos, scores, -jnp.inf)
        top = jnp.max(scores, axis=1, keepdims=True)
        weights = jnp.exp2((scores - top) * exp2_scale)
        total = jnp.sum(weights, axis=1, keepdims=True)
        mixed = dot_nn(weights.astype(jnp.bfloat16), values)
        out[0:rows, h * HD : (h + 1) * HD] = (mixed / total).astype(jnp.bfloat16)
    oq = jnp.concatenate([oq[:, h * HD : (h + 1) * HD] for h in range(heads)], axis=0)
    step = lax.rem(lax.broadcasted_iota(jnp.int32, (heads * opt, 1), 0), opt)
    scores = jnp.where(key_pos > step, dot_nt(oq, keys), -jnp.inf)
    own = dot_nt(oq, own_keys)
    own = jnp.where(lax.broadcasted_iota(jnp.int32, (1, opt), 1) <= step, own, -jnp.inf)
    top = jnp.maximum(
        jnp.max(scores, axis=1, keepdims=True), jnp.max(own, axis=1, keepdims=True)
    )
    weights = jnp.exp2((scores - top) * exp2_scale)
    own = jnp.exp2((own - top) * exp2_scale)
    total = jnp.sum(weights, axis=1, keepdims=True) + jnp.sum(own, axis=1, keepdims=True)
    mixed = dot_nn(weights.astype(jnp.bfloat16), values) + dot_nn(
        own.astype(jnp.bfloat16), own_values
    )
    mixed = (mixed / total).astype(jnp.bfloat16)
    for h in range(heads):
        out[rows : rows + opt, h * HD : (h + 1) * HD] = mixed[h * opt : (h + 1) * opt]


def project_kernel(w0, w1, w2, a0, a1, a2, a3, out, placed):
    z = lax.axis_index("head")
    for t, block in enumerate((a0, a1, a2, a3)):
        placed[z ^ t] = block[...]
    s = lax.axis_index("seq")
    blocks = [placed[(s ^ m) >> 1] for m in masks(s)]
    half = out.shape[0] // 2
    for n in range(2):
        part = slice(n * half, (n + 1) * half)
        total = dot_nt(w0[part, :], blocks[0])
        total += dot_nt(w1[part, :], blocks[1])
        out[part, :] = total + dot_nt(w2[part, :], blocks[2])


def complete_kernel(rows, opt, packed, w3, a0, a1, a2, a3, partial, out, placed):
    z = lax.axis_index("head")
    for t, block in enumerate((a0, a1, a2, a3)):
        placed[z ^ t] = block[...]
    s = lax.axis_index("seq")
    block = placed[(s ^ masks(s)[3]) >> 1]
    features = w3.shape[0]
    half = features // 2
    for n in range(2):
        part = slice(n * half, (n + 1) * half)
        total = partial[part, :] + dot_nt(w3[part, :], block)
        if packed:
            total = total.astype(out.dtype)
            out[part, :] = total[:, 0:rows]
            out[features : features + half, n * opt : (n + 1) * opt] = total[:, rows : rows + opt]
        else:
            out[part, :] = total


def square_kernel(rows, opt, own, received, projected, squares):
    features = own.shape[0]
    half = features // 2
    left = own[:, 0:rows] + received[0:features, :].astype(jnp.float32)
    projected[:, 0:rows] = left
    squares[:, 0:rows] = jnp.sum(left * left, axis=0, keepdims=True)
    total = 0.0
    for n in range(2):
        part = slice(n * half, (n + 1) * half)
        right = received[features : features + half, n * opt : (n + 1) * opt]
        right = own[part, rows : rows + opt] + right.astype(jnp.float32)
        projected[part, rows : rows + opt] = right
        total += jnp.sum(right * right, axis=0, keepdims=True)
    squares[:, rows : rows + opt] = total


def scale_kernel(rows, bounds, projected, gain, prefix, option, kept, share):
    features = prefix.shape[0]
    start, length = bounds[0, 0], bounds[0, 1]
    position = lax.broadcasted_iota(jnp.int32, kept.shape, 0)
    inside = position < length
    count = jnp.zeros(kept.shape, jnp.float32) + (length - start).astype(jnp.float32)
    kept[...] = jnp.where(inside, 1.0, 0.0)
    share[...] = jnp.where(inside & (position >= start), count, 0.0)
    row = gain[...]
    prefix[...] = projected[:, 0:rows] * jnp.broadcast_to(row, (rows, features)).T
    option[...] = projected[:, rows:].T * row


def finish_kernel(
    rows, width, prefix, option, kept, share, s0, s1, s2, s3, resid_t, opt_resid,
    out_t, opt_out, summary, held_t, held_opt, held_sum, sems,
):
    squares = s0[...] + s1[...] + s2[...] + s3[...]
    scale = lax.rsqrt(squares / width + epsilon)
    held_t[...] = (resid_t[...].astype(jnp.float32) + prefix[...] * scale[:, 0:rows]).astype(
        jnp.bfloat16
    )
    copies = [
        pltpu.make_async_copy(a, b, sems.at[i])
        for i, (a, b) in enumerate(((held_t, out_t), (held_opt, opt_out), (held_sum, summary)))
    ]
    copies[0].start()
    opt = opt_resid.shape[1]
    column = jnp.broadcast_to(scale[:, rows : rows + opt], (HD, opt)).T[:, 0:1]
    full = opt_resid[0].astype(jnp.float32) + option[...] * column
    full = jnp.where(kept[:, 0:1] > 0.0, full, 0.0).astype(jnp.bfloat16)
    held_opt[0] = full
    copies[1].start()
    counts = share[:, 0:1]
    chosen = jnp.where(counts > 0.0, full.astype(jnp.float32), 0.0)
    held_sum[...] = jnp.sum(chosen, axis=0, keepdims=True) / jnp.max(counts, axis=0, keepdims=True)
    copies[2].start()
    for copy in copies:
        copy.wait()


def paired_body(
    queries,
    keys,
    values,
    prefix_resid,
    opt_queries,
    opt_keys,
    opt_values,
    opt_resid,
    out_weight,
    norm_gain,
    option_bounds,
):
    rows, opt = queries.shape[0], opt_queries.shape[1]
    features = out_weight.shape[1]
    wide = queries.shape[1] // 2
    seq = range(lax.axis_size("seq"))
    bf16, f32 = jnp.bfloat16, jnp.float32
    shape = jax.ShapeDtypeStruct
    pair = [(s, s ^ 1) for s in seq]
    first = [(s, s ^ (2 if s % 2 else 4)) for s in seq]
    second = [(s, s ^ (4 if s % 2 else 2)) for s in seq]
    both = [(s, s ^ 6) for s in seq]

    def turned(value, steps):
        count = lax.axis_size("head")
        return lax.ppermute(value, "head", [(i, (i + steps) % count) for i in range(count)])

    def after(value, *others):
        return lax.optimization_barrier((value, *others))[0]

    def in_hbm(value):
        return pltpu.with_memory_space_constraint(value, HBM)

    def crossed(value, mask):
        return lax.ppermute(value, "head", [(i, i ^ mask) for i in range(lax.axis_size("head"))])

    weight = out_weight.T

    packed = pltpu.VMEM((2 * rows + 2 * opt, wide), bf16)
    sent, kept = call(
        pack_kernel,
        [packed, packed],
        6,
        in_specs=[pl.BlockSpec(memory_space=HBM)] * 6,
        scratch=[pltpu.SemaphoreType.DMA((12,))],
    )(*map(in_hbm, (queries, keys, values, opt_queries, opt_keys, opt_values)))
    received = lax.ppermute(sent, "seq", pair)
    kv_0 = call(join_kernel, pltpu.VMEM((2 * rows, 2 * HD), bf16), 2)(kept, received)
    slots = (
        kv_0,
        lax.ppermute(kv_0, "seq", first),
        lax.ppermute(kv_0, "seq", second),
        lax.ppermute(kv_0, "seq", both),
    )

    attn_shape = pltpu.VMEM((rows + opt, wide), bf16)

    def attention(flip, block, weight):
        return call(
            functools.partial(attn_kernel, flip, rows, opt),
            attn_shape,
            5,
            flops=weight * 4 * (rows + opt) * wide * WINDOW,
            vmem=24,
        )(*slots, block)

    pair_0 = attention(1, received, LONG_P)
    own_0 = attention(0, kept, LONG_O)
    pair_1, pair_2 = crossed(pair_0, 1), crossed(pair_0, 2)
    own_1, own_2 = crossed(own_0, 1), crossed(own_0, 2)
    pair_3 = crossed(after(pair_2, own_0), 1)
    own_3 = crossed(own_2, 1)

    weight_1 = lax.ppermute(after(weight, received), "seq", first)
    weight_2 = lax.ppermute(after(weight, pair_0), "seq", second)
    weight_3 = lax.ppermute(after(weight_1, own_0), "seq", second)
    flops = 2 * features * wide * (rows + opt)
    placed = [pltpu.VMEM((4, rows + opt, wide), bf16)]

    def project(blocks):
        return call(
            project_kernel,
            shape((features, rows + opt), f32),
            7,
            flops=LONG_M * 3 * flops,
            scratch=placed,
            vmem=16,
        )(weight, weight_1, weight_2, *blocks)

    def complete(partial, blocks, out_shape, packed):
        return call(
            functools.partial(complete_kernel, rows, opt, packed),
            out_shape,
            6,
            flops=flops,
            scratch=placed,
            vmem=16,
        )(weight_3, *blocks, partial)

    pair_blocks = (after(pair_0, own_1, own_3), pair_1, pair_2, pair_3)
    own_blocks = (own_0, own_1, own_2, own_3)
    pair_part, own_part = project(pair_blocks), project(own_blocks)
    half = complete(
        pair_part, pair_blocks, shape((features + features // 2, rows), bf16), True
    )
    received = lax.ppermute(half, "seq", pair)
    own = complete(own_part, own_blocks, shape((features, rows + opt), f32), False)
    projected, squares = call(
        functools.partial(square_kernel, rows, opt),
        [shape((features, rows + opt), f32), shape((1, rows + opt), f32)],
        2,
    )(own, received)
    scaled = call(
        functools.partial(scale_kernel, rows),
        [shape((features, rows), f32), shape((opt, features), f32)]
        + [shape((opt, HD), f32)] * 2,
        3,
        in_specs=[pl.BlockSpec(memory_space=SMEM)] + [pl.BlockSpec(memory_space=VMEM)] * 2,
    )(option_bounds, projected, norm_gain[None])
    results = [
        shape((features, rows), bf16),
        shape((1, opt, features), bf16),
        shape((1, features), f32),
    ]
    out_t, opt_out, summary = call(
        functools.partial(finish_kernel, rows, float(features * lax.axis_size("head"))),
        results,
        10,
        out_specs=[pl.BlockSpec(memory_space=HBM)] * 3,
        scratch=[pltpu.VMEM(r.shape, r.dtype) for r in results] + [pltpu.SemaphoreType.DMA((3,))],
    )(
        *scaled,
        squares,
        turned(squares, 1),
        turned(squares, 2),
        turned(squares, 3),
        prefix_resid.T,
        opt_resid,
    )
    return out_t.T, opt_out, summary


def body(*args):
    queries, keys, opt_queries, out_weight = args[0], args[1], args[4], args[8]
    seq, head = lax.axis_size("seq"), lax.axis_size("head")
    paired = (
        seq == 8
        and head == 4
        and seq * queries.shape[0] == WINDOW
        and queries.shape[0] == HD
        and queries.shape[0] == 2 * opt_queries.shape[1]
        and keys.shape[1] == 2 * HD
        and out_weight.shape[0] * 2 == queries.shape[1]
        and out_weight.shape[0] * seq == queries.shape[1] * head
    )
    return paired_body(*args) if paired else general_body(*args)


def solution(mesh):
    return jax.shard_map(
        body,
        mesh=mesh,
        in_specs=(
            P("seq", "head"),
            P("seq", "head"),
            P("seq", "head"),
            P("seq", "head"),
            P("seq", None, "head"),
            P("seq", None, "head"),
            P("seq", None, "head"),
            P("seq", None, "head"),
            P("seq", "head"),
            P("head"),
            P("seq", None),
        ),
        out_specs=(P("seq", "head"), P("seq", None, "head"), P("seq", "head")),
        check_vma=False,
    )
```

```python
import functools

import jax
import jax.numpy as jnp
from jax import lax
from jax.experimental import pallas as pl
from jax.experimental.pallas import tpu as pltpu
from jax.sharding import PartitionSpec as P

HD = 128
WINDOW = 1024
score_scale = 168.0 ** (-0.5)
exp2_scale = score_scale * 1.4426950408889634
epsilon = 1e-06


def passed_along(value, axis, steps):
    count = lax.axis_size(axis)
    initial, last = (max(0, -steps), min(count, count - steps))
    return lax.ppermute(value, axis, [(source, source + steps) for source in range(initial, last)])


def from_root(block, axis, owner):
    block = jnp.where(lax.axis_index(axis) == owner, block, jnp.zeros_like(block))
    return lax.psum(block, axis)


def attend(query_rows, key_rows, value_rows, allowed):
    row_count = query_rows.shape[0]
    kv_heads = key_rows.shape[1] // HD
    groups = query_rows.shape[1] // key_rows.shape[1]
    query_view = query_rows.reshape(row_count, kv_heads, groups, HD)
    key_view = key_rows.reshape(-1, kv_heads, HD)
    scores = (
        jnp.einsum("rkgd,lkd->kgrl", query_view, key_view, preferred_element_type=jnp.float32)
        * score_scale
    )
    scores = jnp.where(allowed[None, None], scores, -jnp.inf)
    row_max = jnp.max(scores, axis=-1, keepdims=True)
    weights = jnp.exp(scores - row_max)
    weights = (weights / jnp.sum(weights, axis=-1, keepdims=True)).astype(jnp.bfloat16)
    value_view = value_rows.reshape(-1, kv_heads, HD)
    attended = jnp.einsum("kgrl,lkd->rkgd", weights, value_view, preferred_element_type=jnp.float32)
    return attended.reshape(row_count, -1).astype(jnp.bfloat16)


def general_body(
    queries,
    keys,
    values,
    prefix_resid,
    opt_queries,
    opt_keys,
    opt_values,
    opt_resid,
    out_weight,
    norm_gain,
    option_bounds,
):
    local_rows = queries.shape[0]
    opt_len = opt_queries.shape[1]
    seq_count = lax.axis_size("seq")
    seq_index = lax.axis_index("seq")
    halo_count = WINDOW // local_rows
    earlier_keys = []
    earlier_values = []
    carried = (keys, values)
    for hop_index in range(halo_count):
        carried = passed_along((carried[0], carried[1]), "seq", 1)
        earlier_keys.insert(0, carried[0])
        earlier_values.insert(0, carried[1])
    window_keys = jnp.concatenate(earlier_keys + [keys], axis=0)
    window_values = jnp.concatenate(earlier_values + [values], axis=0)
    query_pos = seq_index * local_rows + jnp.arange(local_rows, dtype=jnp.int32)
    key_pos = (seq_index - halo_count) * local_rows + jnp.arange(
        window_keys.shape[0], dtype=jnp.int32
    )
    allowed = (
        (key_pos[None] <= query_pos[:, None])
        & (key_pos[None] > query_pos[:, None] - WINDOW)
        & (key_pos[None] >= 0)
    )
    prefix_attn = attend(queries, window_keys, window_values, allowed)
    final_keys, final_values = (
        from_root(window_keys[local_rows:], "seq", seq_count - 1),
        from_root(window_values[local_rows:], "seq", seq_count - 1),
    )
    joined_keys = jnp.concatenate([final_keys, opt_keys[0]], axis=0)
    joined_values = jnp.concatenate([final_values, opt_values[0]], axis=0)
    positions = jnp.arange(WINDOW + opt_len, dtype=jnp.int32)
    option_pos = jnp.arange(opt_len, dtype=jnp.int32)
    option_allowed = jnp.where(
        positions[None] < WINDOW,
        positions[None] > option_pos[:, None],
        positions[None] - WINDOW <= option_pos[:, None],
    )
    option_attn = attend(opt_queries[0], joined_keys, joined_values, option_allowed)
    stacked = jnp.concatenate([prefix_attn, option_attn], axis=0)
    weight_share = lax.all_gather(out_weight, "seq", axis=0, tiled=True)
    head_cols = stacked.shape[1]
    attn_whole = lax.all_gather(stacked, "head", axis=1, tiled=True)
    projected = jnp.zeros((stacked.shape[0], weight_share.shape[1]), jnp.float32)
    for group in range(lax.axis_size("head")):
        partial_value = jnp.dot(
            attn_whole[:, group * head_cols : (group + 1) * head_cols],
            weight_share[group * head_cols : (group + 1) * head_cols],
            preferred_element_type=jnp.float32,
        )
        projected = projected + lax.optimization_barrier(partial_value.astype(jnp.bfloat16)).astype(
            jnp.float32
        )
    squares = lax.psum(jnp.sum(projected * projected, axis=1), "head")
    width = norm_gain.shape[0] * lax.axis_size("head")
    normed = projected * lax.rsqrt(squares / width + epsilon)[:, None] * norm_gain[None, :]
    prefix_out = (prefix_resid.astype(jnp.float32) + normed[:local_rows]).astype(jnp.bfloat16)
    option_full = opt_resid[0].astype(jnp.float32) + normed[local_rows:]
    start_pos = option_bounds[0, 0]
    length = option_bounds[0, 1]
    inside = option_pos < length
    option_out = jnp.where(inside[:, None], option_full, 0.0).astype(jnp.bfloat16)
    chosen = inside & (option_pos >= start_pos)
    option_summary = jnp.sum(
        jnp.where(chosen[:, None], option_out.astype(jnp.float32), 0.0), axis=0
    ) / (length - start_pos).astype(jnp.float32)
    return (prefix_out, option_out[None], option_summary[None])


ATTENTION_COST, PROJECTION_COST = 200, 8


SMEM = pltpu.MemorySpace.SMEM
VMEM = pltpu.MemorySpace.VMEM
HBM = pltpu.MemorySpace.HBM


def dot_nt(a, b):
    return lax.dot_general(a, b, (((1,), (1,)), ((), ())), preferred_element_type=jnp.float32)


def dot_nn(a, b):
    return lax.dot_general(a, b, (((1,), (0,)), ((), ())), preferred_element_type=jnp.float32)


def call(kernel, out_shape, count, flops=0, moved=0, in_specs=None, out_specs=None, scratch=(), vmem=8):
    many = isinstance(out_shape, (list, tuple))
    return pl.pallas_call(
        kernel,
        out_shape=out_shape,
        in_specs=in_specs or [pl.BlockSpec(memory_space=VMEM)] * count,
        out_specs=out_specs
        or ([pl.BlockSpec(memory_space=VMEM)] * len(out_shape) if many else pl.BlockSpec(memory_space=VMEM)),
        scratch_shapes=list(scratch),
        cost_estimate=pl.CostEstimate(flops=flops, bytes_accessed=moved, transcendentals=0),
        compiler_params=pltpu.CompilerParams(vmem_limit_bytes=vmem * 1024 * 1024),
    )


def masks(s):
    parity = lax.rem(s, 2)
    return (0 * parity, 4 - 2 * parity, 2 + 2 * parity, 0 * parity + 6)


def pack_kernel(q, k, v, oq, ok, ov, kept, sent, sems):
    parity = lax.rem(lax.axis_index("seq"), 2)
    rows, opt = q.shape[0], oq.shape[1]
    wide = q.shape[1] // 2
    mine = pl.ds(pl.multiple_of(parity * HD, HD), HD)
    pieces = [
        (k.at[:, mine], kept.at[0:rows, 0:HD]),
        (v.at[:, mine], kept.at[0:rows, HD : 2 * HD]),
    ]
    for to, base, head in ((kept, rows, parity), (sent, 0, 1 - parity)):
        at = pl.ds(pl.multiple_of(head * HD, HD), HD)
        at_q = pl.ds(pl.multiple_of(head * wide, wide), wide)
        own = pl.ds(base + rows + opt, opt)
        pieces += [
            (q.at[:, at_q], to.at[base : base + rows, :]),
            (oq.at[0, :, at_q], to.at[base + rows : base + rows + opt, :]),
            (ok.at[0, :, at], to.at[own, 0:HD]),
            (ov.at[0, :, at], to.at[own, HD : 2 * HD]),
        ]
    copies = [pltpu.make_async_copy(a, b, sems.at[i]) for i, (a, b) in enumerate(pieces)]
    for copy in copies:
        copy.start()
    for copy in copies:
        copy.wait()


def join_kernel(kept, k, v, out):
    rows = k.shape[0]
    mine = pl.ds(pl.multiple_of(lax.rem(lax.axis_index("seq"), 2) * HD, HD), HD)
    out[0:rows, :] = kept[0:rows, :]
    out[rows : 2 * rows, 0:HD] = k[:, mine]
    out[rows : 2 * rows, HD : 2 * HD] = v[:, mine]


def attn_kernel(rows, opt, kv0, kv1, kv2, kv3, received, kept, out):
    for flip, base, packed in ((1, 0, received), (0, rows, kept)):
        own = slice(base + rows + opt, base + rows + 2 * opt)
        attn(
            (kv0, kv1, kv2, kv3),
            flip,
            packed[base : base + rows, :],
            packed[base + rows : base + rows + opt, :],
            packed[own, 0:HD],
            packed[own, HD : 2 * HD],
            out.at[(1 - flip) * (rows + opt) : (2 - flip) * (rows + opt), :],
        )


def attn(slots, flip, q, oq, own_keys, own_values, out):
    s = lax.axis_index("seq")
    rows, opt = q.shape[0], oq.shape[0]
    keys = jnp.concatenate([kv[:, 0:HD] for kv in slots], axis=0)
    values = jnp.concatenate([kv[:, HD : 2 * HD] for kv in slots], axis=0)
    lane = lax.broadcasted_iota(jnp.int32, (1, rows), 1)
    key_pos = jnp.concatenate(
        [((s ^ m) ^ b) * rows + lane for m in masks(s) for b in (0, 1)], axis=1
    )
    query_pos = (s ^ flip) * rows + lax.broadcasted_iota(jnp.int32, (rows, 1), 0)
    heads = q.shape[1] // HD
    parts = [x[:, h * HD : (h + 1) * HD] for x in (q, oq) for h in range(heads)]
    scores = dot_nt(jnp.concatenate(parts, axis=0), keys)
    last = heads * rows
    weights = []
    for h in range(heads):
        mine = jnp.where(key_pos <= query_pos, scores[h * rows : (h + 1) * rows], -jnp.inf)
        top = jnp.max(mine, axis=1, keepdims=True)
        weights.append(jnp.exp2((mine - top) * exp2_scale).astype(jnp.bfloat16))
    step = lax.rem(lax.broadcasted_iota(jnp.int32, (heads * opt, 1), 0), opt)
    mine = jnp.where(key_pos > step, scores[last:], -jnp.inf)
    own = dot_nt(jnp.concatenate(parts[heads:], axis=0), own_keys)
    own = jnp.where(lax.broadcasted_iota(jnp.int32, (1, opt), 1) <= step, own, -jnp.inf)
    top = jnp.maximum(jnp.max(mine, axis=1, keepdims=True), jnp.max(own, axis=1, keepdims=True))
    weights.append(jnp.exp2((mine - top) * exp2_scale).astype(jnp.bfloat16))
    own = jnp.exp2((own - top) * exp2_scale).astype(jnp.bfloat16)
    mixed = dot_nn(jnp.concatenate(weights, axis=0), beside_ones(values))
    for h in range(heads):
        rest = mixed[h * rows : (h + 1) * rows]
        out[0:rows, h * HD : (h + 1) * HD] = (rest[:, :HD] / rest[:, HD : HD + 1]).astype(
            jnp.bfloat16
        )
    rest = mixed[last:] + dot_nn(own, beside_ones(own_values))
    rest = (rest[:, :HD] / rest[:, HD : HD + 1]).astype(jnp.bfloat16)
    for h in range(heads):
        out[rows : rows + opt, h * HD : (h + 1) * HD] = rest[h * opt : (h + 1) * opt]


def beside_ones(values):
    return jnp.concatenate([values, jnp.ones_like(values)], axis=1)


def apart():
    s, z = lax.axis_index("seq"), lax.axis_index("head")
    return [((s ^ mask) >> 1) ^ z for mask in masks(s)]


def project_kernel(w0, w1, w2, a0, a1, a2, pair_out, own_out, chosen, placed):
    for t, block in enumerate((a0, a1, a2)):
        placed[t] = block[...]
    placed[3] = jnp.zeros_like(a0)
    meets = apart()
    held = (w0, w1, w2)
    chosen[...] = w0[...]
    for j in (1, 2):

        @pl.when(meets[j] == 3)
        def _():
            chosen[...] = held[j][...]

    count = a0.shape[0] // 2
    middle = w0.shape[0] // 2
    for r, out in enumerate((pair_out, own_out)):
        blocks = [placed[meets[j], r * count : (r + 1) * count, :] for j in range(3)]
        for n in range(2):
            part = slice(n * middle, (n + 1) * middle)
            total = dot_nt(w0[part, :], blocks[0]) + dot_nt(w1[part, :], blocks[1])
            out[part, :] = total + dot_nt(w2[part, :], blocks[2])


def complete_kernel(rows, opt, packed, w3, chosen, a0, a1, a2, a3, partial, out, placed):
    mine = slice(0, rows + opt) if packed else slice(rows + opt, 2 * (rows + opt))
    for t, block in enumerate((a0, a1, a2, a3)):
        placed[t] = block[mine, :]
    meets = apart()[3]
    first = placed[meets]
    second = jnp.where(meets == 3, jnp.zeros_like(first), placed[3])
    features = w3.shape[0]
    half = features // 2
    for n in range(2):
        part = slice(n * half, (n + 1) * half)
        total = dot_nt(w3[part, :], first) + dot_nt(chosen[part, :], second)
        total += partial[part, :]
        if packed:
            total = total.astype(out.dtype)
            out[part, :] = total[:, 0:rows]
            out[features : features + half, n * opt : (n + 1) * opt] = total[:, rows : rows + opt]
        else:
            out[part, :] = total


def square_kernel(rows, opt, own, received, projected, squares):
    features = own.shape[0]
    half = features // 2
    left = own[:, 0:rows] + received[0:features, :].astype(jnp.float32)
    projected[:, 0:rows] = left
    squares[:, 0:rows] = jnp.sum(left * left, axis=0, keepdims=True)
    total = 0.0
    for n in range(2):
        part = slice(n * half, (n + 1) * half)
        right = received[features : features + half, n * opt : (n + 1) * opt]
        right = own[part, rows : rows + opt] + right.astype(jnp.float32)
        projected[part, rows : rows + opt] = right
        total += jnp.sum(right * right, axis=0, keepdims=True)
    squares[:, rows : rows + opt] = total


def scale_kernel(rows, bounds, projected, gain, prefix, option, kept, share):
    features = prefix.shape[0]
    start, length = bounds[0, 0], bounds[0, 1]
    position = lax.broadcasted_iota(jnp.int32, kept.shape, 0)
    inside = position < length
    count = jnp.zeros(kept.shape, jnp.float32) + (length - start).astype(jnp.float32)
    kept[...] = jnp.where(inside, 1.0, 0.0)
    share[...] = jnp.where(inside & (position >= start), count, 0.0)
    row = gain[...]
    prefix[...] = projected[:, 0:rows] * jnp.broadcast_to(row, (rows, features)).T
    option[...] = projected[:, rows:].T * row


def finish_kernel(
    rows, width, prefix, option, kept, share, s0, s1, s2, s3, resid_t, opt_resid,
    out_t, opt_out, summary, held_t, held_opt, held_sum, sems,
):
    squares = s0[...] + s1[...] + s2[...] + s3[...]
    scale = lax.rsqrt(squares / width + epsilon)
    held_t[...] = (resid_t[...].astype(jnp.float32) + prefix[...] * scale[:, 0:rows]).astype(
        jnp.bfloat16
    )
    copies = [
        pltpu.make_async_copy(a, b, sems.at[i])
        for i, (a, b) in enumerate(((held_t, out_t), (held_opt, opt_out), (held_sum, summary)))
    ]
    copies[0].start()
    opt = opt_resid.shape[1]
    column = jnp.broadcast_to(scale[:, rows : rows + opt], (HD, opt)).T[:, 0:1]
    full = opt_resid[0].astype(jnp.float32) + option[...] * column
    full = jnp.where(kept[:, 0:1] > 0.0, full, 0.0).astype(jnp.bfloat16)
    held_opt[0] = full
    copies[1].start()
    counts = share[:, 0:1]
    chosen = jnp.where(counts > 0.0, full.astype(jnp.float32), 0.0)
    held_sum[...] = jnp.sum(chosen, axis=0, keepdims=True) / jnp.max(counts, axis=0, keepdims=True)
    copies[2].start()
    for copy in copies:
        copy.wait()


def paired_body(
    queries,
    keys,
    values,
    prefix_resid,
    opt_queries,
    opt_keys,
    opt_values,
    opt_resid,
    out_weight,
    norm_gain,
    option_bounds,
):
    rows, opt = queries.shape[0], opt_queries.shape[1]
    features = out_weight.shape[1]
    wide = queries.shape[1] // 2
    seq = range(lax.axis_size("seq"))
    bf16, f32 = jnp.bfloat16, jnp.float32
    shape = jax.ShapeDtypeStruct
    pair = [(s, s ^ 1) for s in seq]
    first = [(s, s ^ (2 if s % 2 else 4)) for s in seq]
    second = [(s, s ^ (4 if s % 2 else 2)) for s in seq]
    both = [(s, s ^ 6) for s in seq]

    def turned(value, steps):
        count = lax.axis_size("head")
        return lax.ppermute(value, "head", [(i, (i + steps) % count) for i in range(count)])

    def after(value, *others):
        return lax.optimization_barrier((value, *others))[0]

    def in_hbm(value):
        return pltpu.with_memory_space_constraint(value, HBM)

    def crossed(value, mask):
        return lax.ppermute(value, "head", [(i, i ^ mask) for i in range(lax.axis_size("head"))])

    weight = out_weight.T

    pair_k = lax.ppermute(keys, "seq", pair)
    pair_v = lax.ppermute(values, "seq", pair)
    kept, sent = call(
        pack_kernel,
        [pltpu.VMEM((2 * rows + 2 * opt, wide), bf16), pltpu.VMEM((rows + 2 * opt, wide), bf16)],
        6,
        in_specs=[pl.BlockSpec(memory_space=HBM)] * 6,
        scratch=[pltpu.SemaphoreType.DMA((10,))],
    )(*map(in_hbm, (queries, keys, values, opt_queries, opt_keys, opt_values)))
    kv_0 = call(join_kernel, pltpu.VMEM((2 * rows, 2 * HD), bf16), 3)(kept, pair_k, pair_v)
    received = lax.ppermute(after(sent, kv_0), "seq", pair)
    kv_3 = lax.ppermute(kv_0, "seq", both)
    kv_1 = lax.ppermute(kv_0, "seq", first)
    kv_2 = lax.ppermute(kv_0, "seq", second)
    slots = (kv_0, kv_1, kv_2, kv_3)

    block = call(
        functools.partial(attn_kernel, rows, opt),
        pltpu.VMEM((2 * (rows + opt), wide), bf16),
        6,
        flops=ATTENTION_COST * 4 * (rows + opt) * wide * WINDOW,
        vmem=24,
    )(*slots, received, kept)
    block_1, block_2 = crossed(block, 1), crossed(block, 2)
    blocks = (block, block_1, block_2, crossed(block_2, 1))

    weight_1 = lax.ppermute(after(weight, kv_0), "seq", first)
    weight_2 = lax.ppermute(after(weight, block), "seq", second)
    weight_3 = lax.ppermute(after(weight_1, block), "seq", second)
    flops = 4 * features * wide * (rows + opt)
    pair_part, own_part, chosen = call(
        project_kernel,
        [shape((features, rows + opt), f32)] * 2 + [shape((features, wide), bf16)],
        6,
        flops=PROJECTION_COST * 3 * flops,
        scratch=[pltpu.VMEM((4, 2 * (rows + opt), wide), bf16)],
        vmem=16,
    )(weight, weight_1, weight_2, *blocks[:3])

    def complete(partial, out_shape, packed):
        return call(
            functools.partial(complete_kernel, rows, opt, packed),
            out_shape,
            7,
            flops=flops // 2,
            scratch=[pltpu.VMEM((4, rows + opt, wide), bf16)],
            vmem=16,
        )(weight_3, chosen, *blocks, partial)

    half = complete(pair_part, shape((features + features // 2, rows), bf16), True)
    received = lax.ppermute(half, "seq", pair)
    own = complete(own_part, shape((features, rows + opt), f32), False)
    projected, squares = call(
        functools.partial(square_kernel, rows, opt),
        [shape((features, rows + opt), f32), shape((1, rows + opt), f32)],
        2,
    )(own, received)
    scaled = call(
        functools.partial(scale_kernel, rows),
        [shape((features, rows), f32), shape((opt, features), f32)]
        + [shape((opt, HD), f32)] * 2,
        3,
        in_specs=[pl.BlockSpec(memory_space=SMEM)] + [pl.BlockSpec(memory_space=VMEM)] * 2,
    )(option_bounds, projected, norm_gain[None])
    results = [
        shape((features, rows), bf16),
        shape((1, opt, features), bf16),
        shape((1, features), f32),
    ]
    out_t, opt_out, summary = call(
        functools.partial(finish_kernel, rows, float(features * lax.axis_size("head"))),
        results,
        10,
        out_specs=[pl.BlockSpec(memory_space=HBM)] * 3,
        scratch=[pltpu.VMEM(r.shape, r.dtype) for r in results] + [pltpu.SemaphoreType.DMA((3,))],
    )(
        *scaled,
        squares,
        turned(squares, 1),
        turned(squares, 2),
        turned(squares, 3),
        prefix_resid.T,
        opt_resid,
    )
    return out_t.T, opt_out, summary


def body(*args):
    queries, keys, opt_queries, out_weight = args[0], args[1], args[4], args[8]
    seq, head = lax.axis_size("seq"), lax.axis_size("head")
    paired = (
        seq == 8
        and head == 4
        and seq * queries.shape[0] == WINDOW
        and queries.shape[0] == HD
        and queries.shape[0] == 2 * opt_queries.shape[1]
        and keys.shape[1] == 2 * HD
        and out_weight.shape[0] * 2 == queries.shape[1]
        and out_weight.shape[0] * seq == queries.shape[1] * head
    )
    return paired_body(*args) if paired else general_body(*args)


def solution(mesh):
    return jax.shard_map(
        body,
        mesh=mesh,
        in_specs=(
            P("seq", "head"),
            P("seq", "head"),
            P("seq", "head"),
            P("seq", "head"),
            P("seq", None, "head"),
            P("seq", None, "head"),
            P("seq", None, "head"),
            P("seq", None, "head"),
            P("seq", "head"),
            P("head"),
            P("seq", None),
        ),
        out_specs=(P("seq", "head"), P("seq", None, "head"), P("seq", "head")),
        check_vma=False,
    )
```

```python
import functools

import jax
import jax.numpy as jnp
from jax import lax
from jax.experimental import pallas as pl
from jax.experimental.pallas import tpu as pltpu
from jax.sharding import PartitionSpec as P

HD = 128
WINDOW = 1024
score_scale = 168.0 ** (-0.5)
exp2_scale = score_scale * 1.4426950408889634
epsilon = 1e-06


def passed_along(value, axis, steps):
    count = lax.axis_size(axis)
    initial, last = (max(0, -steps), min(count, count - steps))
    return lax.ppermute(value, axis, [(source, source + steps) for source in range(initial, last)])


def from_root(block, axis, owner):
    block = jnp.where(lax.axis_index(axis) == owner, block, jnp.zeros_like(block))
    return lax.psum(block, axis)


def attend(query_rows, key_rows, value_rows, allowed):
    row_count = query_rows.shape[0]
    kv_heads = key_rows.shape[1] // HD
    groups = query_rows.shape[1] // key_rows.shape[1]
    query_view = query_rows.reshape(row_count, kv_heads, groups, HD)
    key_view = key_rows.reshape(-1, kv_heads, HD)
    scores = (
        jnp.einsum("rkgd,lkd->kgrl", query_view, key_view, preferred_element_type=jnp.float32)
        * score_scale
    )
    scores = jnp.where(allowed[None, None], scores, -jnp.inf)
    row_max = jnp.max(scores, axis=-1, keepdims=True)
    weights = jnp.exp(scores - row_max)
    weights = (weights / jnp.sum(weights, axis=-1, keepdims=True)).astype(jnp.bfloat16)
    value_view = value_rows.reshape(-1, kv_heads, HD)
    attended = jnp.einsum("kgrl,lkd->rkgd", weights, value_view, preferred_element_type=jnp.float32)
    return attended.reshape(row_count, -1).astype(jnp.bfloat16)


def general_body(
    queries,
    keys,
    values,
    prefix_resid,
    opt_queries,
    opt_keys,
    opt_values,
    opt_resid,
    out_weight,
    norm_gain,
    option_bounds,
):
    local_rows = queries.shape[0]
    opt_len = opt_queries.shape[1]
    seq_count = lax.axis_size("seq")
    seq_index = lax.axis_index("seq")
    halo_count = WINDOW // local_rows
    earlier_keys = []
    earlier_values = []
    carried = (keys, values)
    for hop_index in range(halo_count):
        carried = passed_along((carried[0], carried[1]), "seq", 1)
        earlier_keys.insert(0, carried[0])
        earlier_values.insert(0, carried[1])
    window_keys = jnp.concatenate(earlier_keys + [keys], axis=0)
    window_values = jnp.concatenate(earlier_values + [values], axis=0)
    query_pos = seq_index * local_rows + jnp.arange(local_rows, dtype=jnp.int32)
    key_pos = (seq_index - halo_count) * local_rows + jnp.arange(
        window_keys.shape[0], dtype=jnp.int32
    )
    allowed = (
        (key_pos[None] <= query_pos[:, None])
        & (key_pos[None] > query_pos[:, None] - WINDOW)
        & (key_pos[None] >= 0)
    )
    prefix_attn = attend(queries, window_keys, window_values, allowed)
    final_keys, final_values = (
        from_root(window_keys[local_rows:], "seq", seq_count - 1),
        from_root(window_values[local_rows:], "seq", seq_count - 1),
    )
    joined_keys = jnp.concatenate([final_keys, opt_keys[0]], axis=0)
    joined_values = jnp.concatenate([final_values, opt_values[0]], axis=0)
    positions = jnp.arange(WINDOW + opt_len, dtype=jnp.int32)
    option_pos = jnp.arange(opt_len, dtype=jnp.int32)
    option_allowed = jnp.where(
        positions[None] < WINDOW,
        positions[None] > option_pos[:, None],
        positions[None] - WINDOW <= option_pos[:, None],
    )
    option_attn = attend(opt_queries[0], joined_keys, joined_values, option_allowed)
    stacked = jnp.concatenate([prefix_attn, option_attn], axis=0)
    weight_share = lax.all_gather(out_weight, "seq", axis=0, tiled=True)
    head_cols = stacked.shape[1]
    attn_whole = lax.all_gather(stacked, "head", axis=1, tiled=True)
    projected = jnp.zeros((stacked.shape[0], weight_share.shape[1]), jnp.float32)
    for group in range(lax.axis_size("head")):
        partial_value = jnp.dot(
            attn_whole[:, group * head_cols : (group + 1) * head_cols],
            weight_share[group * head_cols : (group + 1) * head_cols],
            preferred_element_type=jnp.float32,
        )
        projected = projected + lax.optimization_barrier(partial_value.astype(jnp.bfloat16)).astype(
            jnp.float32
        )
    squares = lax.psum(jnp.sum(projected * projected, axis=1), "head")
    width = norm_gain.shape[0] * lax.axis_size("head")
    normed = projected * lax.rsqrt(squares / width + epsilon)[:, None] * norm_gain[None, :]
    prefix_out = (prefix_resid.astype(jnp.float32) + normed[:local_rows]).astype(jnp.bfloat16)
    option_full = opt_resid[0].astype(jnp.float32) + normed[local_rows:]
    start_pos = option_bounds[0, 0]
    length = option_bounds[0, 1]
    inside = option_pos < length
    option_out = jnp.where(inside[:, None], option_full, 0.0).astype(jnp.bfloat16)
    chosen = inside & (option_pos >= start_pos)
    option_summary = jnp.sum(
        jnp.where(chosen[:, None], option_out.astype(jnp.float32), 0.0), axis=0
    ) / (length - start_pos).astype(jnp.float32)
    return (prefix_out, option_out[None], option_summary[None])


ATTENTION_COST, PROJECTION_COST = 200, 8


SMEM = pltpu.MemorySpace.SMEM
VMEM = pltpu.MemorySpace.VMEM
HBM = pltpu.MemorySpace.HBM


def dot_nt(a, b):
    return lax.dot_general(a, b, (((1,), (1,)), ((), ())), preferred_element_type=jnp.float32)


def dot_nn(a, b):
    return lax.dot_general(a, b, (((1,), (0,)), ((), ())), preferred_element_type=jnp.float32)


def call(kernel, out_shape, count, flops=0, moved=0, in_specs=None, out_specs=None, scratch=(), vmem=8):
    many = isinstance(out_shape, (list, tuple))
    return pl.pallas_call(
        kernel,
        out_shape=out_shape,
        in_specs=in_specs or [pl.BlockSpec(memory_space=VMEM)] * count,
        out_specs=out_specs
        or ([pl.BlockSpec(memory_space=VMEM)] * len(out_shape) if many else pl.BlockSpec(memory_space=VMEM)),
        scratch_shapes=list(scratch),
        cost_estimate=pl.CostEstimate(flops=flops, bytes_accessed=moved, transcendentals=0),
        compiler_params=pltpu.CompilerParams(vmem_limit_bytes=vmem * 1024 * 1024),
    )


def masks(s):
    parity = lax.rem(s, 2)
    return (0 * parity, 4 - 2 * parity, 2 + 2 * parity, 0 * parity + 6)


def pack_kernel(q, k, v, oq, ok, ov, kept, sent, sems):
    parity = lax.rem(lax.axis_index("seq"), 2)
    rows, opt = q.shape[0], oq.shape[1]
    wide = q.shape[1] // 2
    mine = pl.ds(pl.multiple_of(parity * HD, HD), HD)
    pieces = [
        (k.at[:, mine], kept.at[0:rows, 0:HD]),
        (v.at[:, mine], kept.at[0:rows, HD : 2 * HD]),
    ]
    for to, base, head in ((kept, rows, parity), (sent, 0, 1 - parity)):
        at = pl.ds(pl.multiple_of(head * HD, HD), HD)
        at_q = pl.ds(pl.multiple_of(head * wide, wide), wide)
        own = pl.ds(base + rows + opt, opt)
        pieces += [
            (q.at[:, at_q], to.at[base : base + rows, :]),
            (oq.at[0, :, at_q], to.at[base + rows : base + rows + opt, :]),
            (ok.at[0, :, at], to.at[own, 0:HD]),
            (ov.at[0, :, at], to.at[own, HD : 2 * HD]),
        ]
    copies = [pltpu.make_async_copy(a, b, sems.at[i]) for i, (a, b) in enumerate(pieces)]
    for copy in copies:
        copy.start()
    for copy in copies:
        copy.wait()


def join_kernel(kept, k, v, out):
    rows = k.shape[0]
    mine = pl.ds(pl.multiple_of(lax.rem(lax.axis_index("seq"), 2) * HD, HD), HD)
    out[0:rows, :] = kept[0:rows, :]
    out[rows : 2 * rows, 0:HD] = k[:, mine]
    out[rows : 2 * rows, HD : 2 * HD] = v[:, mine]


def attn_kernel(rows, opt, kv0, kv3, kv1, kv2, received, kept, out):
    for flip, base, packed in ((1, 0, received), (0, rows, kept)):
        own = slice(base + rows + opt, base + rows + 2 * opt)
        attn(
            (kv0, kv1, kv2, kv3),
            flip,
            packed[base : base + rows, :],
            packed[base + rows : base + rows + opt, :],
            packed[own, 0:HD],
            packed[own, HD : 2 * HD],
            out.at[(1 - flip) * (rows + opt) : (2 - flip) * (rows + opt), :],
        )


def attn(slots, flip, q, oq, own_keys, own_values, out):
    s = lax.axis_index("seq")
    rows, opt = q.shape[0], oq.shape[0]
    keys = jnp.concatenate([kv[:, 0:HD] for kv in slots], axis=0)
    values = jnp.concatenate([kv[:, HD : 2 * HD] for kv in slots], axis=0)
    lane = lax.broadcasted_iota(jnp.int32, (1, rows), 1)
    key_pos = jnp.concatenate(
        [((s ^ m) ^ b) * rows + lane for m in masks(s) for b in (0, 1)], axis=1
    )
    query_pos = (s ^ flip) * rows + lax.broadcasted_iota(jnp.int32, (rows, 1), 0)
    heads = q.shape[1] // HD
    parts = [x[:, h * HD : (h + 1) * HD] for x in (q, oq) for h in range(heads)]
    scores = dot_nt(jnp.concatenate(parts, axis=0), keys)
    last = heads * rows
    weights = []
    for h in range(heads):
        mine = jnp.where(key_pos <= query_pos, scores[h * rows : (h + 1) * rows], -jnp.inf)
        top = jnp.max(mine, axis=1, keepdims=True)
        weights.append(jnp.exp2((mine - top) * exp2_scale).astype(jnp.bfloat16))
    step = lax.rem(lax.broadcasted_iota(jnp.int32, (heads * opt, 1), 0), opt)
    mine = jnp.where(key_pos > step, scores[last:], -jnp.inf)
    own = dot_nt(jnp.concatenate(parts[heads:], axis=0), own_keys)
    own = jnp.where(lax.broadcasted_iota(jnp.int32, (1, opt), 1) <= step, own, -jnp.inf)
    top = jnp.maximum(jnp.max(mine, axis=1, keepdims=True), jnp.max(own, axis=1, keepdims=True))
    weights.append(jnp.exp2((mine - top) * exp2_scale).astype(jnp.bfloat16))
    own = jnp.exp2((own - top) * exp2_scale).astype(jnp.bfloat16)
    mixed = dot_nn(jnp.concatenate(weights, axis=0), beside_ones(values))
    for h in range(heads):
        rest = mixed[h * rows : (h + 1) * rows]
        out[0:rows, h * HD : (h + 1) * HD] = (rest[:, :HD] / rest[:, HD : HD + 1]).astype(
            jnp.bfloat16
        )
    rest = mixed[last:] + dot_nn(own, beside_ones(own_values))
    rest = (rest[:, :HD] / rest[:, HD : HD + 1]).astype(jnp.bfloat16)
    for h in range(heads):
        out[rows : rows + opt, h * HD : (h + 1) * HD] = rest[h * opt : (h + 1) * opt]


def beside_ones(values):
    return jnp.concatenate([values, jnp.ones_like(values)], axis=1)


def apart():
    s, z = lax.axis_index("seq"), lax.axis_index("head")
    return [((s ^ mask) >> 1) ^ z for mask in masks(s)]


def project_kernel(w0, w1, w2, a0, a1, a2, pair_out, own_out, chosen, placed):
    for t, block in enumerate((a0, a1, a2)):
        placed[t] = block[...]
    placed[3] = jnp.zeros_like(a0)
    meets = apart()
    held = (w0, w1, w2)
    chosen[...] = w0[...]
    for j in (1, 2):

        @pl.when(meets[j] == 3)
        def _():
            chosen[...] = held[j][...]

    count = a0.shape[0] // 2
    middle = w0.shape[0] // 2
    for r, out in enumerate((pair_out, own_out)):
        blocks = [placed[meets[j], r * count : (r + 1) * count, :] for j in range(3)]
        for n in range(2):
            part = slice(n * middle, (n + 1) * middle)
            total = dot_nt(w0[part, :], blocks[0]) + dot_nt(w1[part, :], blocks[1])
            out[part, :] = total + dot_nt(w2[part, :], blocks[2])


def complete_kernel(rows, opt, packed, w3, chosen, a0, a1, a2, a3, partial, out, placed):
    mine = slice(0, rows + opt) if packed else slice(rows + opt, 2 * (rows + opt))
    for t, block in enumerate((a0, a1, a2, a3)):
        placed[t] = block[mine, :]
    meets = apart()[3]
    first = placed[meets]
    second = jnp.where(meets == 3, jnp.zeros_like(first), placed[3])
    features = w3.shape[0]
    half = features // 2
    for n in range(2):
        part = slice(n * half, (n + 1) * half)
        total = dot_nt(w3[part, :], first) + dot_nt(chosen[part, :], second)
        total += partial[part, :]
        if packed:
            total = total.astype(out.dtype)
            out[part, :] = total[:, 0:rows]
            out[features : features + half, n * opt : (n + 1) * opt] = total[:, rows : rows + opt]
        else:
            out[part, :] = total


def square_kernel(rows, opt, own, received, projected, squares):
    features = own.shape[0]
    half = features // 2
    left = own[:, 0:rows] + received[0:features, :].astype(jnp.float32)
    projected[:, 0:rows] = left
    squares[:, 0:rows] = jnp.sum(left * left, axis=0, keepdims=True)
    total = 0.0
    for n in range(2):
        part = slice(n * half, (n + 1) * half)
        right = received[features : features + half, n * opt : (n + 1) * opt]
        right = own[part, rows : rows + opt] + right.astype(jnp.float32)
        projected[part, rows : rows + opt] = right
        total += jnp.sum(right * right, axis=0, keepdims=True)
    squares[:, rows : rows + opt] = total


def scale_kernel(rows, bounds, projected, gain, prefix, option, kept, share):
    features = prefix.shape[0]
    start, length = bounds[0, 0], bounds[0, 1]
    position = lax.broadcasted_iota(jnp.int32, kept.shape, 0)
    inside = position < length
    count = jnp.zeros(kept.shape, jnp.float32) + (length - start).astype(jnp.float32)
    kept[...] = jnp.where(inside, 1.0, 0.0)
    share[...] = jnp.where(inside & (position >= start), count, 0.0)
    row = gain[...]
    prefix[...] = projected[:, 0:rows] * jnp.broadcast_to(row, (rows, features)).T
    option[...] = projected[:, rows:].T * row


def finish_kernel(
    rows, width, prefix, option, kept, share, s0, s1, s2, s3, resid_t, opt_resid,
    out_t, opt_out, summary, held_t, held_opt, held_sum, sems,
):
    squares = s0[...] + s1[...] + s2[...] + s3[...]
    scale = lax.rsqrt(squares / width + epsilon)
    held_t[...] = (resid_t[...].astype(jnp.float32) + prefix[...] * scale[:, 0:rows]).astype(
        jnp.bfloat16
    )
    copies = [
        pltpu.make_async_copy(a, b, sems.at[i])
        for i, (a, b) in enumerate(((held_t, out_t), (held_opt, opt_out), (held_sum, summary)))
    ]
    copies[0].start()
    opt = opt_resid.shape[1]
    column = jnp.broadcast_to(scale[:, rows : rows + opt], (HD, opt)).T[:, 0:1]
    full = opt_resid[0].astype(jnp.float32) + option[...] * column
    full = jnp.where(kept[:, 0:1] > 0.0, full, 0.0).astype(jnp.bfloat16)
    held_opt[0] = full
    copies[1].start()
    counts = share[:, 0:1]
    chosen = jnp.where(counts > 0.0, full.astype(jnp.float32), 0.0)
    held_sum[...] = jnp.sum(chosen, axis=0, keepdims=True) / jnp.max(counts, axis=0, keepdims=True)
    copies[2].start()
    for copy in copies:
        copy.wait()


def paired_body(
    queries,
    keys,
    values,
    prefix_resid,
    opt_queries,
    opt_keys,
    opt_values,
    opt_resid,
    out_weight,
    norm_gain,
    option_bounds,
):
    rows, opt = queries.shape[0], opt_queries.shape[1]
    features = out_weight.shape[1]
    wide = queries.shape[1] // 2
    seq = range(lax.axis_size("seq"))
    bf16, f32 = jnp.bfloat16, jnp.float32
    shape = jax.ShapeDtypeStruct
    pair = [(s, s ^ 1) for s in seq]
    first = [(s, s ^ (2 if s % 2 else 4)) for s in seq]
    second = [(s, s ^ (4 if s % 2 else 2)) for s in seq]
    both = [(s, s ^ 6) for s in seq]

    def turned(value, steps):
        count = lax.axis_size("head")
        return lax.ppermute(value, "head", [(i, (i + steps) % count) for i in range(count)])

    def after(value, *others):
        return lax.optimization_barrier((value, *others))[0]

    def in_hbm(value):
        return pltpu.with_memory_space_constraint(value, HBM)

    def crossed(value, mask):
        return lax.ppermute(value, "head", [(i, i ^ mask) for i in range(lax.axis_size("head"))])

    weight = out_weight.T

    pair_k = lax.ppermute(keys, "seq", pair)
    pair_v = lax.ppermute(values, "seq", pair)
    kept, sent = call(
        pack_kernel,
        [pltpu.VMEM((2 * rows + 2 * opt, wide), bf16), pltpu.VMEM((rows + 2 * opt, wide), bf16)],
        6,
        in_specs=[pl.BlockSpec(memory_space=HBM)] * 6,
        scratch=[pltpu.SemaphoreType.DMA((10,))],
    )(*map(in_hbm, (queries, keys, values, opt_queries, opt_keys, opt_values)))
    kv_0 = call(join_kernel, pltpu.VMEM((2 * rows, 2 * HD), bf16), 3)(kept, pair_k, pair_v)
    received = lax.ppermute(after(sent, kv_0), "seq", pair)
    kv_3 = lax.ppermute(kv_0, "seq", both)
    kv_1 = lax.ppermute(kv_0, "seq", first)
    kv_2 = lax.ppermute(kv_0, "seq", second)
    slots = (kv_0, kv_3, kv_1, kv_2)

    block = call(
        functools.partial(attn_kernel, rows, opt),
        pltpu.VMEM((2 * (rows + opt), wide), bf16),
        6,
        flops=ATTENTION_COST * 4 * (rows + opt) * wide * WINDOW,
        vmem=24,
    )(*slots, received, kept)
    block_1, block_2 = crossed(block, 1), crossed(block, 2)
    blocks = (block, block_1, block_2, crossed(block_2, 1))

    weight_1 = lax.ppermute(after(weight, kv_0), "seq", first)
    weight_2 = lax.ppermute(after(weight, block), "seq", second)
    weight_3 = lax.ppermute(after(weight_1, block), "seq", second)
    flops = 4 * features * wide * (rows + opt)
    pair_part, own_part, chosen = call(
        project_kernel,
        [shape((features, rows + opt), f32)] * 2 + [shape((features, wide), bf16)],
        6,
        flops=PROJECTION_COST * 3 * flops,
        scratch=[pltpu.VMEM((4, 2 * (rows + opt), wide), bf16)],
        vmem=16,
    )(weight, weight_1, weight_2, *blocks[:3])

    def complete(partial, out_shape, packed):
        return call(
            functools.partial(complete_kernel, rows, opt, packed),
            out_shape,
            7,
            flops=flops // 2,
            scratch=[pltpu.VMEM((4, rows + opt, wide), bf16)],
            vmem=16,
        )(weight_3, chosen, *blocks, partial)

    half = complete(pair_part, shape((features + features // 2, rows), bf16), True)
    received = lax.ppermute(half, "seq", pair)
    own = complete(own_part, shape((features, rows + opt), f32), False)
    projected, squares = call(
        functools.partial(square_kernel, rows, opt),
        [shape((features, rows + opt), f32), shape((1, rows + opt), f32)],
        2,
    )(own, received)
    scaled = call(
        functools.partial(scale_kernel, rows),
        [shape((features, rows), f32), shape((opt, features), f32)]
        + [shape((opt, HD), f32)] * 2,
        3,
        in_specs=[pl.BlockSpec(memory_space=SMEM)] + [pl.BlockSpec(memory_space=VMEM)] * 2,
    )(option_bounds, projected, norm_gain[None])
    results = [
        shape((features, rows), bf16),
        shape((1, opt, features), bf16),
        shape((1, features), f32),
    ]
    out_t, opt_out, summary = call(
        functools.partial(finish_kernel, rows, float(features * lax.axis_size("head"))),
        results,
        10,
        out_specs=[pl.BlockSpec(memory_space=HBM)] * 3,
        scratch=[pltpu.VMEM(r.shape, r.dtype) for r in results] + [pltpu.SemaphoreType.DMA((3,))],
    )(
        *scaled,
        squares,
        turned(squares, 1),
        turned(squares, 2),
        turned(squares, 3),
        prefix_resid.T,
        opt_resid,
    )
    return out_t.T, opt_out, summary


def body(*args):
    queries, keys, opt_queries, out_weight = args[0], args[1], args[4], args[8]
    seq, head = lax.axis_size("seq"), lax.axis_size("head")
    paired = (
        seq == 8
        and head == 4
        and seq * queries.shape[0] == WINDOW
        and queries.shape[0] == HD
        and queries.shape[0] == 2 * opt_queries.shape[1]
        and keys.shape[1] == 2 * HD
        and out_weight.shape[0] * 2 == queries.shape[1]
        and out_weight.shape[0] * seq == queries.shape[1] * head
    )
    return paired_body(*args) if paired else general_body(*args)


def solution(mesh):
    return jax.shard_map(
        body,
        mesh=mesh,
        in_specs=(
            P("seq", "head"),
            P("seq", "head"),
            P("seq", "head"),
            P("seq", "head"),
            P("seq", None, "head"),
            P("seq", None, "head"),
            P("seq", None, "head"),
            P("seq", None, "head"),
            P("seq", "head"),
            P("head"),
            P("seq", None),
        ),
        out_specs=(P("seq", "head"), P("seq", None, "head"), P("seq", "head")),
        check_vma=False,
    )
```

```python
import functools

import jax
import jax.numpy as jnp
from jax import lax
from jax.experimental import pallas as pl
from jax.experimental.pallas import tpu as pltpu
from jax.sharding import PartitionSpec as P

HD = 128
WINDOW = 1024
score_scale = 168.0 ** (-0.5)
exp2_scale = score_scale * 1.4426950408889634
epsilon = 1e-06


def passed_along(value, axis, steps):
    count = lax.axis_size(axis)
    initial, last = (max(0, -steps), min(count, count - steps))
    return lax.ppermute(value, axis, [(source, source + steps) for source in range(initial, last)])


def from_root(block, axis, owner):
    block = jnp.where(lax.axis_index(axis) == owner, block, jnp.zeros_like(block))
    return lax.psum(block, axis)


def attend(query_rows, key_rows, value_rows, allowed):
    row_count = query_rows.shape[0]
    kv_heads = key_rows.shape[1] // HD
    groups = query_rows.shape[1] // key_rows.shape[1]
    query_view = query_rows.reshape(row_count, kv_heads, groups, HD)
    key_view = key_rows.reshape(-1, kv_heads, HD)
    scores = (
        jnp.einsum("rkgd,lkd->kgrl", query_view, key_view, preferred_element_type=jnp.float32)
        * score_scale
    )
    scores = jnp.where(allowed[None, None], scores, -jnp.inf)
    row_max = jnp.max(scores, axis=-1, keepdims=True)
    weights = jnp.exp(scores - row_max)
    weights = (weights / jnp.sum(weights, axis=-1, keepdims=True)).astype(jnp.bfloat16)
    value_view = value_rows.reshape(-1, kv_heads, HD)
    attended = jnp.einsum("kgrl,lkd->rkgd", weights, value_view, preferred_element_type=jnp.float32)
    return attended.reshape(row_count, -1).astype(jnp.bfloat16)


def general_body(
    queries,
    keys,
    values,
    prefix_resid,
    opt_queries,
    opt_keys,
    opt_values,
    opt_resid,
    out_weight,
    norm_gain,
    option_bounds,
):
    local_rows = queries.shape[0]
    opt_len = opt_queries.shape[1]
    seq_count = lax.axis_size("seq")
    seq_index = lax.axis_index("seq")
    halo_count = WINDOW // local_rows
    earlier_keys = []
    earlier_values = []
    carried = (keys, values)
    for hop_index in range(halo_count):
        carried = passed_along((carried[0], carried[1]), "seq", 1)
        earlier_keys.insert(0, carried[0])
        earlier_values.insert(0, carried[1])
    window_keys = jnp.concatenate(earlier_keys + [keys], axis=0)
    window_values = jnp.concatenate(earlier_values + [values], axis=0)
    query_pos = seq_index * local_rows + jnp.arange(local_rows, dtype=jnp.int32)
    key_pos = (seq_index - halo_count) * local_rows + jnp.arange(
        window_keys.shape[0], dtype=jnp.int32
    )
    allowed = (
        (key_pos[None] <= query_pos[:, None])
        & (key_pos[None] > query_pos[:, None] - WINDOW)
        & (key_pos[None] >= 0)
    )
    prefix_attn = attend(queries, window_keys, window_values, allowed)
    final_keys, final_values = (
        from_root(window_keys[local_rows:], "seq", seq_count - 1),
        from_root(window_values[local_rows:], "seq", seq_count - 1),
    )
    joined_keys = jnp.concatenate([final_keys, opt_keys[0]], axis=0)
    joined_values = jnp.concatenate([final_values, opt_values[0]], axis=0)
    positions = jnp.arange(WINDOW + opt_len, dtype=jnp.int32)
    option_pos = jnp.arange(opt_len, dtype=jnp.int32)
    option_allowed = jnp.where(
        positions[None] < WINDOW,
        positions[None] > option_pos[:, None],
        positions[None] - WINDOW <= option_pos[:, None],
    )
    option_attn = attend(opt_queries[0], joined_keys, joined_values, option_allowed)
    stacked = jnp.concatenate([prefix_attn, option_attn], axis=0)
    weight_share = lax.all_gather(out_weight, "seq", axis=0, tiled=True)
    head_cols = stacked.shape[1]
    attn_whole = lax.all_gather(stacked, "head", axis=1, tiled=True)
    projected = jnp.zeros((stacked.shape[0], weight_share.shape[1]), jnp.float32)
    for group in range(lax.axis_size("head")):
        partial_value = jnp.dot(
            attn_whole[:, group * head_cols : (group + 1) * head_cols],
            weight_share[group * head_cols : (group + 1) * head_cols],
            preferred_element_type=jnp.float32,
        )
        projected = projected + lax.optimization_barrier(partial_value.astype(jnp.bfloat16)).astype(
            jnp.float32
        )
    squares = lax.psum(jnp.sum(projected * projected, axis=1), "head")
    width = norm_gain.shape[0] * lax.axis_size("head")
    normed = projected * lax.rsqrt(squares / width + epsilon)[:, None] * norm_gain[None, :]
    prefix_out = (prefix_resid.astype(jnp.float32) + normed[:local_rows]).astype(jnp.bfloat16)
    option_full = opt_resid[0].astype(jnp.float32) + normed[local_rows:]
    start_pos = option_bounds[0, 0]
    length = option_bounds[0, 1]
    inside = option_pos < length
    option_out = jnp.where(inside[:, None], option_full, 0.0).astype(jnp.bfloat16)
    chosen = inside & (option_pos >= start_pos)
    option_summary = jnp.sum(
        jnp.where(chosen[:, None], option_out.astype(jnp.float32), 0.0), axis=0
    ) / (length - start_pos).astype(jnp.float32)
    return (prefix_out, option_out[None], option_summary[None])


ATTENTION_COST, PROJECTION_COST = 200, 5


SMEM = pltpu.MemorySpace.SMEM
VMEM = pltpu.MemorySpace.VMEM
HBM = pltpu.MemorySpace.HBM


def dot_nt(a, b):
    return lax.dot_general(a, b, (((1,), (1,)), ((), ())), preferred_element_type=jnp.float32)


def dot_nn(a, b):
    return lax.dot_general(a, b, (((1,), (0,)), ((), ())), preferred_element_type=jnp.float32)


def call(kernel, out_shape, count, flops=0, moved=0, in_specs=None, out_specs=None, scratch=(), vmem=8):
    many = isinstance(out_shape, (list, tuple))
    return pl.pallas_call(
        kernel,
        out_shape=out_shape,
        in_specs=in_specs or [pl.BlockSpec(memory_space=VMEM)] * count,
        out_specs=out_specs
        or ([pl.BlockSpec(memory_space=VMEM)] * len(out_shape) if many else pl.BlockSpec(memory_space=VMEM)),
        scratch_shapes=list(scratch),
        cost_estimate=pl.CostEstimate(flops=flops, bytes_accessed=moved, transcendentals=0),
        compiler_params=pltpu.CompilerParams(vmem_limit_bytes=vmem * 1024 * 1024),
    )


def masks(s):
    parity = lax.rem(s, 2)
    return (0 * parity, 4 - 2 * parity, 2 + 2 * parity, 0 * parity + 6)


def pack_kernel(q, k, v, oq, ok, ov, kept, sent, sems):
    parity = lax.rem(lax.axis_index("seq"), 2)
    rows, opt = q.shape[0], oq.shape[1]
    wide = q.shape[1] // 2
    mine = pl.ds(pl.multiple_of(parity * HD, HD), HD)
    pieces = [
        (k.at[:, mine], kept.at[0:rows, 0:HD]),
        (v.at[:, mine], kept.at[0:rows, HD : 2 * HD]),
    ]
    for to, base, head in ((kept, rows, parity), (sent, 0, 1 - parity)):
        at = pl.ds(pl.multiple_of(head * HD, HD), HD)
        at_q = pl.ds(pl.multiple_of(head * wide, wide), wide)
        own = pl.ds(base + rows + opt, opt)
        pieces += [
            (q.at[:, at_q], to.at[base : base + rows, :]),
            (oq.at[0, :, at_q], to.at[base + rows : base + rows + opt, :]),
            (ok.at[0, :, at], to.at[own, 0:HD]),
            (ov.at[0, :, at], to.at[own, HD : 2 * HD]),
        ]
    copies = [pltpu.make_async_copy(a, b, sems.at[i]) for i, (a, b) in enumerate(pieces)]
    for copy in copies:
        copy.start()
    for copy in copies:
        copy.wait()


def join_kernel(kept, k, v, out):
    rows = k.shape[0]
    mine = pl.ds(pl.multiple_of(lax.rem(lax.axis_index("seq"), 2) * HD, HD), HD)
    out[0:rows, :] = kept[0:rows, :]
    out[rows : 2 * rows, 0:HD] = k[:, mine]
    out[rows : 2 * rows, HD : 2 * HD] = v[:, mine]


def attn_kernel(rows, opt, kv0, kv3, kv1, kv2, received, kept, out):
    for flip, base, packed in ((1, 0, received), (0, rows, kept)):
        own = slice(base + rows + opt, base + rows + 2 * opt)
        attn(
            (kv0, kv1, kv2, kv3),
            flip,
            packed[base : base + rows, :],
            packed[base + rows : base + rows + opt, :],
            packed[own, 0:HD],
            packed[own, HD : 2 * HD],
            out.at[(1 - flip) * (rows + opt) : (2 - flip) * (rows + opt), :],
        )


def attn(slots, flip, q, oq, own_keys, own_values, out):
    s = lax.axis_index("seq")
    rows, opt = q.shape[0], oq.shape[0]
    keys = jnp.concatenate([kv[:, 0:HD] for kv in slots], axis=0)
    values = jnp.concatenate([kv[:, HD : 2 * HD] for kv in slots], axis=0)
    lane = lax.broadcasted_iota(jnp.int32, (1, rows), 1)
    key_pos = jnp.concatenate(
        [((s ^ m) ^ b) * rows + lane for m in masks(s) for b in (0, 1)], axis=1
    )
    query_pos = (s ^ flip) * rows + lax.broadcasted_iota(jnp.int32, (rows, 1), 0)
    heads = q.shape[1] // HD
    parts = [x[:, h * HD : (h + 1) * HD] for x in (q, oq) for h in range(heads)]
    scores = dot_nt(jnp.concatenate(parts, axis=0), keys)
    last = heads * rows
    weights = []
    for h in range(heads):
        mine = jnp.where(key_pos <= query_pos, scores[h * rows : (h + 1) * rows], -jnp.inf)
        top = jnp.max(mine, axis=1, keepdims=True)
        weights.append(jnp.exp2((mine - top) * exp2_scale).astype(jnp.bfloat16))
    step = lax.rem(lax.broadcasted_iota(jnp.int32, (heads * opt, 1), 0), opt)
    mine = jnp.where(key_pos > step, scores[last:], -jnp.inf)
    own = dot_nt(jnp.concatenate(parts[heads:], axis=0), own_keys)
    own = jnp.where(lax.broadcasted_iota(jnp.int32, (1, opt), 1) <= step, own, -jnp.inf)
    top = jnp.maximum(jnp.max(mine, axis=1, keepdims=True), jnp.max(own, axis=1, keepdims=True))
    weights.append(jnp.exp2((mine - top) * exp2_scale).astype(jnp.bfloat16))
    own = jnp.exp2((own - top) * exp2_scale).astype(jnp.bfloat16)
    mixed = dot_nn(jnp.concatenate(weights, axis=0), beside_ones(values))
    for h in range(heads):
        rest = mixed[h * rows : (h + 1) * rows]
        out[0:rows, h * HD : (h + 1) * HD] = (rest[:, :HD] / rest[:, HD : HD + 1]).astype(
            jnp.bfloat16
        )
    rest = mixed[last:] + dot_nn(own, beside_ones(own_values))
    rest = (rest[:, :HD] / rest[:, HD : HD + 1]).astype(jnp.bfloat16)
    for h in range(heads):
        out[rows : rows + opt, h * HD : (h + 1) * HD] = rest[h * opt : (h + 1) * opt]


def beside_ones(values):
    return jnp.concatenate([values, jnp.ones_like(values)], axis=1)


def apart():
    s, z = lax.axis_index("seq"), lax.axis_index("head")
    return [((s ^ mask) >> 1) ^ z for mask in masks(s)]


def project_kernel(w0, w1, w2, a0, a1, a2, a3, pair_out, own_out, placed):
    for t, block in enumerate((a0, a1, a2, a3)):
        placed[t] = block[...]
    meets = apart()
    count = a0.shape[0] // 2
    middle = w0.shape[0] // 2
    for r, out in enumerate((pair_out, own_out)):
        blocks = [placed[meets[j], r * count : (r + 1) * count, :] for j in range(3)]
        for n in range(2):
            part = slice(n * middle, (n + 1) * middle)
            total = dot_nt(w0[part, :], blocks[0]) + dot_nt(w1[part, :], blocks[1])
            out[part, :] = total + dot_nt(w2[part, :], blocks[2])


def complete_kernel(rows, opt, packed, w3, a0, a1, a2, a3, partial, out, placed):
    mine = slice(0, rows + opt) if packed else slice(rows + opt, 2 * (rows + opt))
    for t, block in enumerate((a0, a1, a2, a3)):
        placed[t] = block[mine, :]
    block = placed[apart()[3]]
    features = w3.shape[0]
    half = features // 2
    for n in range(2):
        part = slice(n * half, (n + 1) * half)
        total = partial[part, :] + dot_nt(w3[part, :], block)
        if packed:
            total = total.astype(out.dtype)
            out[part, :] = total[:, 0:rows]
            out[features : features + half, n * opt : (n + 1) * opt] = total[:, rows : rows + opt]
        else:
            out[part, :] = total


def square_kernel(rows, opt, own, received, projected, squares):
    features = own.shape[0]
    half = features // 2
    left = own[:, 0:rows] + received[0:features, :].astype(jnp.float32)
    projected[:, 0:rows] = left
    squares[:, 0:rows] = jnp.sum(left * left, axis=0, keepdims=True)
    total = 0.0
    for n in range(2):
        part = slice(n * half, (n + 1) * half)
        right = received[features : features + half, n * opt : (n + 1) * opt]
        right = own[part, rows : rows + opt] + right.astype(jnp.float32)
        projected[part, rows : rows + opt] = right
        total += jnp.sum(right * right, axis=0, keepdims=True)
    squares[:, rows : rows + opt] = total


def scale_kernel(rows, bounds, projected, gain, prefix, option, kept, share):
    features = prefix.shape[0]
    start, length = bounds[0, 0], bounds[0, 1]
    position = lax.broadcasted_iota(jnp.int32, kept.shape, 0)
    inside = position < length
    count = jnp.zeros(kept.shape, jnp.float32) + (length - start).astype(jnp.float32)
    kept[...] = jnp.where(inside, 1.0, 0.0)
    share[...] = jnp.where(inside & (position >= start), count, 0.0)
    row = gain[...]
    prefix[...] = projected[:, 0:rows] * jnp.broadcast_to(row, (rows, features)).T
    option[...] = projected[:, rows:].T * row


def finish_kernel(
    rows, width, prefix, option, kept, share, s0, s1, s2, s3, resid_t, opt_resid,
    out_t, opt_out, summary, held_t, held_opt, held_sum, sems,
):
    squares = s0[...] + s1[...] + s2[...] + s3[...]
    scale = lax.rsqrt(squares / width + epsilon)
    held_t[...] = (resid_t[...].astype(jnp.float32) + prefix[...] * scale[:, 0:rows]).astype(
        jnp.bfloat16
    )
    copies = [
        pltpu.make_async_copy(a, b, sems.at[i])
        for i, (a, b) in enumerate(((held_t, out_t), (held_opt, opt_out), (held_sum, summary)))
    ]
    copies[0].start()
    opt = opt_resid.shape[1]
    column = jnp.broadcast_to(scale[:, rows : rows + opt], (HD, opt)).T[:, 0:1]
    full = opt_resid[0].astype(jnp.float32) + option[...] * column
    full = jnp.where(kept[:, 0:1] > 0.0, full, 0.0).astype(jnp.bfloat16)
    held_opt[0] = full
    copies[1].start()
    counts = share[:, 0:1]
    chosen = jnp.where(counts > 0.0, full.astype(jnp.float32), 0.0)
    held_sum[...] = jnp.sum(chosen, axis=0, keepdims=True) / jnp.max(counts, axis=0, keepdims=True)
    copies[2].start()
    for copy in copies:
        copy.wait()


def paired_body(
    queries,
    keys,
    values,
    prefix_resid,
    opt_queries,
    opt_keys,
    opt_values,
    opt_resid,
    out_weight,
    norm_gain,
    option_bounds,
):
    rows, opt = queries.shape[0], opt_queries.shape[1]
    features = out_weight.shape[1]
    wide = queries.shape[1] // 2
    seq = range(lax.axis_size("seq"))
    bf16, f32 = jnp.bfloat16, jnp.float32
    shape = jax.ShapeDtypeStruct
    pair = [(s, s ^ 1) for s in seq]
    first = [(s, s ^ (2 if s % 2 else 4)) for s in seq]
    second = [(s, s ^ (4 if s % 2 else 2)) for s in seq]
    both = [(s, s ^ 6) for s in seq]

    def turned(value, steps):
        count = lax.axis_size("head")
        return lax.ppermute(value, "head", [(i, (i + steps) % count) for i in range(count)])

    def after(value, *others):
        return lax.optimization_barrier((value, *others))[0]

    def in_hbm(value):
        return pltpu.with_memory_space_constraint(value, HBM)

    def crossed(value, mask):
        return lax.ppermute(value, "head", [(i, i ^ mask) for i in range(lax.axis_size("head"))])

    weight = out_weight.T

    pair_k = lax.ppermute(keys, "seq", pair)
    pair_v = lax.ppermute(values, "seq", pair)
    kept, sent = call(
        pack_kernel,
        [pltpu.VMEM((2 * rows + 2 * opt, wide), bf16), pltpu.VMEM((rows + 2 * opt, wide), bf16)],
        6,
        in_specs=[pl.BlockSpec(memory_space=HBM)] * 6,
        scratch=[pltpu.SemaphoreType.DMA((10,))],
    )(*map(in_hbm, (queries, keys, values, opt_queries, opt_keys, opt_values)))
    kv_0 = call(join_kernel, pltpu.VMEM((2 * rows, 2 * HD), bf16), 3)(kept, pair_k, pair_v)
    received = lax.ppermute(after(sent, kv_0), "seq", pair)
    kv_3 = lax.ppermute(kv_0, "seq", both)
    kv_1 = lax.ppermute(kv_0, "seq", first)
    kv_2 = lax.ppermute(kv_0, "seq", second)
    slots = (kv_0, kv_3, kv_1, kv_2)

    block = call(
        functools.partial(attn_kernel, rows, opt),
        pltpu.VMEM((2 * (rows + opt), wide), bf16),
        6,
        flops=ATTENTION_COST * 4 * (rows + opt) * wide * WINDOW,
        vmem=24,
    )(*slots, received, kept)
    block_1, block_2 = crossed(block, 1), crossed(block, 2)
    blocks = (block, block_1, block_2, crossed(block_2, 1))

    weight_1 = lax.ppermute(after(weight, kv_0), "seq", first)
    weight_2 = lax.ppermute(after(weight, block), "seq", second)
    weight_3 = lax.ppermute(after(weight_1, block), "seq", second)
    flops = 4 * features * wide * (rows + opt)
    pair_part, own_part = call(
        project_kernel,
        [shape((features, rows + opt), f32)] * 2,
        7,
        flops=PROJECTION_COST * 3 * flops,
        scratch=[pltpu.VMEM((4, 2 * (rows + opt), wide), bf16)],
        vmem=16,
    )(weight, weight_1, weight_2, *blocks)

    def complete(partial, out_shape, packed):
        return call(
            functools.partial(complete_kernel, rows, opt, packed),
            out_shape,
            6,
            flops=flops // 2,
            scratch=[pltpu.VMEM((4, rows + opt, wide), bf16)],
            vmem=16,
        )(weight_3, *blocks, partial)

    half = complete(pair_part, shape((features + features // 2, rows), bf16), True)
    received = lax.ppermute(half, "seq", pair)
    own = complete(own_part, shape((features, rows + opt), f32), False)
    projected, squares = call(
        functools.partial(square_kernel, rows, opt),
        [shape((features, rows + opt), f32), shape((1, rows + opt), f32)],
        2,
    )(own, received)
    scaled = call(
        functools.partial(scale_kernel, rows),
        [shape((features, rows), f32), shape((opt, features), f32)]
        + [shape((opt, HD), f32)] * 2,
        3,
        in_specs=[pl.BlockSpec(memory_space=SMEM)] + [pl.BlockSpec(memory_space=VMEM)] * 2,
    )(option_bounds, projected, norm_gain[None])
    results = [
        shape((features, rows), bf16),
        shape((1, opt, features), bf16),
        shape((1, features), f32),
    ]
    out_t, opt_out, summary = call(
        functools.partial(finish_kernel, rows, float(features * lax.axis_size("head"))),
        results,
        10,
        out_specs=[pl.BlockSpec(memory_space=HBM)] * 3,
        scratch=[pltpu.VMEM(r.shape, r.dtype) for r in results] + [pltpu.SemaphoreType.DMA((3,))],
    )(
        *scaled,
        squares,
        turned(squares, 1),
        turned(squares, 2),
        turned(squares, 3),
        prefix_resid.T,
        opt_resid,
    )
    return out_t.T, opt_out, summary


def body(*args):
    queries, keys, opt_queries, out_weight = args[0], args[1], args[4], args[8]
    seq, head = lax.axis_size("seq"), lax.axis_size("head")
    paired = (
        seq == 8
        and head == 4
        and seq * queries.shape[0] == WINDOW
        and queries.shape[0] == HD
        and queries.shape[0] == 2 * opt_queries.shape[1]
        and keys.shape[1] == 2 * HD
        and out_weight.shape[0] * 2 == queries.shape[1]
        and out_weight.shape[0] * seq == queries.shape[1] * head
    )
    return paired_body(*args) if paired else general_body(*args)


def solution(mesh):
    return jax.shard_map(
        body,
        mesh=mesh,
        in_specs=(
            P("seq", "head"),
            P("seq", "head"),
            P("seq", "head"),
            P("seq", "head"),
            P("seq", None, "head"),
            P("seq", None, "head"),
            P("seq", None, "head"),
            P("seq", None, "head"),
            P("seq", "head"),
            P("head"),
            P("seq", None),
        ),
        out_specs=(P("seq", "head"), P("seq", None, "head"), P("seq", "head")),
        check_vma=False,
    )
```

```python
import functools

import jax
import jax.numpy as jnp
from jax import lax
from jax.experimental import pallas as pl
from jax.experimental.pallas import tpu as pltpu
from jax.sharding import PartitionSpec as P

HD = 128
WINDOW = 1024
score_scale = 168.0 ** (-0.5)
exp2_scale = score_scale * 1.4426950408889634
epsilon = 1e-06


def passed_along(value, axis, steps):
    count = lax.axis_size(axis)
    initial, last = (max(0, -steps), min(count, count - steps))
    return lax.ppermute(value, axis, [(source, source + steps) for source in range(initial, last)])


def from_root(block, axis, owner):
    block = jnp.where(lax.axis_index(axis) == owner, block, jnp.zeros_like(block))
    return lax.psum(block, axis)


def attend(query_rows, key_rows, value_rows, allowed):
    row_count = query_rows.shape[0]
    kv_heads = key_rows.shape[1] // HD
    groups = query_rows.shape[1] // key_rows.shape[1]
    query_view = query_rows.reshape(row_count, kv_heads, groups, HD)
    key_view = key_rows.reshape(-1, kv_heads, HD)
    scores = (
        jnp.einsum("rkgd,lkd->kgrl", query_view, key_view, preferred_element_type=jnp.float32)
        * score_scale
    )
    scores = jnp.where(allowed[None, None], scores, -jnp.inf)
    row_max = jnp.max(scores, axis=-1, keepdims=True)
    weights = jnp.exp(scores - row_max)
    weights = (weights / jnp.sum(weights, axis=-1, keepdims=True)).astype(jnp.bfloat16)
    value_view = value_rows.reshape(-1, kv_heads, HD)
    attended = jnp.einsum("kgrl,lkd->rkgd", weights, value_view, preferred_element_type=jnp.float32)
    return attended.reshape(row_count, -1).astype(jnp.bfloat16)


def general_body(
    queries,
    keys,
    values,
    prefix_resid,
    opt_queries,
    opt_keys,
    opt_values,
    opt_resid,
    out_weight,
    norm_gain,
    option_bounds,
):
    local_rows = queries.shape[0]
    opt_len = opt_queries.shape[1]
    seq_count = lax.axis_size("seq")
    seq_index = lax.axis_index("seq")
    halo_count = WINDOW // local_rows
    earlier_keys = []
    earlier_values = []
    carried = (keys, values)
    for hop_index in range(halo_count):
        carried = passed_along((carried[0], carried[1]), "seq", 1)
        earlier_keys.insert(0, carried[0])
        earlier_values.insert(0, carried[1])
    window_keys = jnp.concatenate(earlier_keys + [keys], axis=0)
    window_values = jnp.concatenate(earlier_values + [values], axis=0)
    query_pos = seq_index * local_rows + jnp.arange(local_rows, dtype=jnp.int32)
    key_pos = (seq_index - halo_count) * local_rows + jnp.arange(
        window_keys.shape[0], dtype=jnp.int32
    )
    allowed = (
        (key_pos[None] <= query_pos[:, None])
        & (key_pos[None] > query_pos[:, None] - WINDOW)
        & (key_pos[None] >= 0)
    )
    prefix_attn = attend(queries, window_keys, window_values, allowed)
    final_keys, final_values = (
        from_root(window_keys[local_rows:], "seq", seq_count - 1),
        from_root(window_values[local_rows:], "seq", seq_count - 1),
    )
    joined_keys = jnp.concatenate([final_keys, opt_keys[0]], axis=0)
    joined_values = jnp.concatenate([final_values, opt_values[0]], axis=0)
    positions = jnp.arange(WINDOW + opt_len, dtype=jnp.int32)
    option_pos = jnp.arange(opt_len, dtype=jnp.int32)
    option_allowed = jnp.where(
        positions[None] < WINDOW,
        positions[None] > option_pos[:, None],
        positions[None] - WINDOW <= option_pos[:, None],
    )
    option_attn = attend(opt_queries[0], joined_keys, joined_values, option_allowed)
    stacked = jnp.concatenate([prefix_attn, option_attn], axis=0)
    weight_share = lax.all_gather(out_weight, "seq", axis=0, tiled=True)
    head_cols = stacked.shape[1]
    attn_whole = lax.all_gather(stacked, "head", axis=1, tiled=True)
    projected = jnp.zeros((stacked.shape[0], weight_share.shape[1]), jnp.float32)
    for group in range(lax.axis_size("head")):
        partial_value = jnp.dot(
            attn_whole[:, group * head_cols : (group + 1) * head_cols],
            weight_share[group * head_cols : (group + 1) * head_cols],
            preferred_element_type=jnp.float32,
        )
        projected = projected + lax.optimization_barrier(partial_value.astype(jnp.bfloat16)).astype(
            jnp.float32
        )
    squares = lax.psum(jnp.sum(projected * projected, axis=1), "head")
    width = norm_gain.shape[0] * lax.axis_size("head")
    normed = projected * lax.rsqrt(squares / width + epsilon)[:, None] * norm_gain[None, :]
    prefix_out = (prefix_resid.astype(jnp.float32) + normed[:local_rows]).astype(jnp.bfloat16)
    option_full = opt_resid[0].astype(jnp.float32) + normed[local_rows:]
    start_pos = option_bounds[0, 0]
    length = option_bounds[0, 1]
    inside = option_pos < length
    option_out = jnp.where(inside[:, None], option_full, 0.0).astype(jnp.bfloat16)
    chosen = inside & (option_pos >= start_pos)
    option_summary = jnp.sum(
        jnp.where(chosen[:, None], option_out.astype(jnp.float32), 0.0), axis=0
    ) / (length - start_pos).astype(jnp.float32)
    return (prefix_out, option_out[None], option_summary[None])


ATTENTION_COST, PROJECTION_COST = 200, 8


SMEM = pltpu.MemorySpace.SMEM
VMEM = pltpu.MemorySpace.VMEM
HBM = pltpu.MemorySpace.HBM


def dot_nt(a, b):
    return lax.dot_general(a, b, (((1,), (1,)), ((), ())), preferred_element_type=jnp.float32)


def dot_nn(a, b):
    return lax.dot_general(a, b, (((1,), (0,)), ((), ())), preferred_element_type=jnp.float32)


def call(kernel, out_shape, count, flops=0, moved=0, in_specs=None, out_specs=None, scratch=(), vmem=8):
    many = isinstance(out_shape, (list, tuple))
    return pl.pallas_call(
        kernel,
        out_shape=out_shape,
        in_specs=in_specs or [pl.BlockSpec(memory_space=VMEM)] * count,
        out_specs=out_specs
        or ([pl.BlockSpec(memory_space=VMEM)] * len(out_shape) if many else pl.BlockSpec(memory_space=VMEM)),
        scratch_shapes=list(scratch),
        cost_estimate=pl.CostEstimate(flops=flops, bytes_accessed=moved, transcendentals=0),
        compiler_params=pltpu.CompilerParams(vmem_limit_bytes=vmem * 1024 * 1024),
    )


def masks(s):
    parity = lax.rem(s, 2)
    return (0 * parity, 4 - 2 * parity, 2 + 2 * parity, 0 * parity + 6)


def pack_kernel(q, k, v, oq, ok, ov, kept, sent, sems):
    parity = lax.rem(lax.axis_index("seq"), 2)
    rows, opt = q.shape[0], oq.shape[1]
    wide = q.shape[1] // 2
    mine = pl.ds(pl.multiple_of(parity * HD, HD), HD)
    pieces = [
        (k.at[:, mine], kept.at[0:rows, 0:HD]),
        (v.at[:, mine], kept.at[0:rows, HD : 2 * HD]),
    ]
    for to, base, head in ((kept, rows, parity), (sent, 0, 1 - parity)):
        at = pl.ds(pl.multiple_of(head * HD, HD), HD)
        at_q = pl.ds(pl.multiple_of(head * wide, wide), wide)
        own = pl.ds(base + rows + opt, opt)
        pieces += [
            (q.at[:, at_q], to.at[base : base + rows, :]),
            (oq.at[0, :, at_q], to.at[base + rows : base + rows + opt, :]),
            (ok.at[0, :, at], to.at[own, 0:HD]),
            (ov.at[0, :, at], to.at[own, HD : 2 * HD]),
        ]
    copies = [pltpu.make_async_copy(a, b, sems.at[i]) for i, (a, b) in enumerate(pieces)]
    for copy in copies:
        copy.start()
    for copy in copies:
        copy.wait()


def join_kernel(kept, k, v, out):
    rows = k.shape[0]
    mine = pl.ds(pl.multiple_of(lax.rem(lax.axis_index("seq"), 2) * HD, HD), HD)
    out[0:rows, :] = kept[0:rows, :]
    out[rows : 2 * rows, 0:HD] = k[:, mine]
    out[rows : 2 * rows, HD : 2 * HD] = v[:, mine]


def attn_kernel(rows, opt, kv0, kv3, kv1, kv2, received, kept, out):
    for flip, base, packed in ((1, 0, received), (0, rows, kept)):
        own = slice(base + rows + opt, base + rows + 2 * opt)
        attn(
            (kv0, kv1, kv2, kv3),
            flip,
            packed[base : base + rows, :],
            packed[base + rows : base + rows + opt, :],
            packed[own, 0:HD],
            packed[own, HD : 2 * HD],
            out.at[(1 - flip) * (rows + opt) : (2 - flip) * (rows + opt), :],
        )


def attn(slots, flip, q, oq, own_keys, own_values, out):
    s = lax.axis_index("seq")
    rows, opt = q.shape[0], oq.shape[0]
    keys = jnp.concatenate([kv[:, 0:HD] for kv in slots], axis=0)
    values = jnp.concatenate([kv[:, HD : 2 * HD] for kv in slots], axis=0)
    lane = lax.broadcasted_iota(jnp.int32, (1, rows), 1)
    key_pos = jnp.concatenate(
        [((s ^ m) ^ b) * rows + lane for m in masks(s) for b in (0, 1)], axis=1
    )
    query_pos = (s ^ flip) * rows + lax.broadcasted_iota(jnp.int32, (rows, 1), 0)
    heads = q.shape[1] // HD
    parts = [x[:, h * HD : (h + 1) * HD] for x in (q, oq) for h in range(heads)]
    scores = dot_nt(jnp.concatenate(parts, axis=0), keys)
    last = heads * rows
    weights = []
    for h in range(heads):
        mine = jnp.where(key_pos <= query_pos, scores[h * rows : (h + 1) * rows], -jnp.inf)
        top = jnp.max(mine, axis=1, keepdims=True)
        weights.append(jnp.exp2((mine - top) * exp2_scale).astype(jnp.bfloat16))
    step = lax.rem(lax.broadcasted_iota(jnp.int32, (heads * opt, 1), 0), opt)
    mine = jnp.where(key_pos > step, scores[last:], -jnp.inf)
    own = dot_nt(jnp.concatenate(parts[heads:], axis=0), own_keys)
    own = jnp.where(lax.broadcasted_iota(jnp.int32, (1, opt), 1) <= step, own, -jnp.inf)
    top = jnp.maximum(jnp.max(mine, axis=1, keepdims=True), jnp.max(own, axis=1, keepdims=True))
    weights.append(jnp.exp2((mine - top) * exp2_scale).astype(jnp.bfloat16))
    own = jnp.exp2((own - top) * exp2_scale).astype(jnp.bfloat16)
    mixed = dot_nn(jnp.concatenate(weights, axis=0), beside_ones(values))
    for h in range(heads):
        rest = mixed[h * rows : (h + 1) * rows]
        out[0:rows, h * HD : (h + 1) * HD] = (rest[:, :HD] / rest[:, HD : HD + 1]).astype(
            jnp.bfloat16
        )
    rest = mixed[last:] + dot_nn(own, beside_ones(own_values))
    rest = (rest[:, :HD] / rest[:, HD : HD + 1]).astype(jnp.bfloat16)
    for h in range(heads):
        out[rows : rows + opt, h * HD : (h + 1) * HD] = rest[h * opt : (h + 1) * opt]


def beside_ones(values):
    return jnp.concatenate([values, jnp.ones_like(values)], axis=1)


def apart():
    s, z = lax.axis_index("seq"), lax.axis_index("head")
    return [((s ^ mask) >> 1) ^ z for mask in masks(s)]


def project_kernel(w0, w1, w2, a0, a1, a2, pair_out, own_out, chosen, placed):
    for t, block in enumerate((a0, a1, a2)):
        placed[t] = block[...]
    placed[3] = jnp.zeros_like(a0)
    meets = apart()
    held = (w0, w1, w2)
    chosen[...] = w0[...]
    for j in (1, 2):

        @pl.when(meets[j] == 3)
        def _():
            chosen[...] = held[j][...]

    count = a0.shape[0] // 2
    middle = w0.shape[0] // 2
    for r, out in enumerate((pair_out, own_out)):
        blocks = [placed[meets[j], r * count : (r + 1) * count, :] for j in range(3)]
        for n in range(2):
            part = slice(n * middle, (n + 1) * middle)
            total = dot_nt(w0[part, :], blocks[0]) + dot_nt(w1[part, :], blocks[1])
            out[part, :] = total + dot_nt(w2[part, :], blocks[2])


def add_kernel(chosen, a3, pair_part, own_part, pair_out, own_out):
    block = a3[...]
    block = jnp.where(apart()[3] == 3, jnp.zeros_like(block), block)
    count = block.shape[0] // 2
    middle = chosen.shape[0] // 2
    for r, (part, out) in enumerate(((pair_part, pair_out), (own_part, own_out))):
        for n in range(2):
            at = slice(n * middle, (n + 1) * middle)
            product = dot_nt(chosen[at, :], block[r * count : (r + 1) * count, :])
            out[at, :] = part[at, :] + product


def complete_kernel(rows, opt, packed, w3, a0, a1, a2, a3, partial, out, placed):
    mine = slice(0, rows + opt) if packed else slice(rows + opt, 2 * (rows + opt))
    for t, block in enumerate((a0, a1, a2, a3)):
        placed[t] = block[mine, :]
    block = placed[apart()[3]]
    features = w3.shape[0]
    half = features // 2
    for n in range(2):
        part = slice(n * half, (n + 1) * half)
        total = partial[part, :] + dot_nt(w3[part, :], block)
        if packed:
            total = total.astype(out.dtype)
            out[part, :] = total[:, 0:rows]
            out[features : features + half, n * opt : (n + 1) * opt] = total[:, rows : rows + opt]
        else:
            out[part, :] = total


def square_kernel(rows, opt, own, received, projected, squares):
    features = own.shape[0]
    half = features // 2
    left = own[:, 0:rows] + received[0:features, :].astype(jnp.float32)
    projected[:, 0:rows] = left
    squares[:, 0:rows] = jnp.sum(left * left, axis=0, keepdims=True)
    total = 0.0
    for n in range(2):
        part = slice(n * half, (n + 1) * half)
        right = received[features : features + half, n * opt : (n + 1) * opt]
        right = own[part, rows : rows + opt] + right.astype(jnp.float32)
        projected[part, rows : rows + opt] = right
        total += jnp.sum(right * right, axis=0, keepdims=True)
    squares[:, rows : rows + opt] = total


def scale_kernel(rows, bounds, projected, gain, prefix, option, kept, share):
    features = prefix.shape[0]
    start, length = bounds[0, 0], bounds[0, 1]
    position = lax.broadcasted_iota(jnp.int32, kept.shape, 0)
    inside = position < length
    count = jnp.zeros(kept.shape, jnp.float32) + (length - start).astype(jnp.float32)
    kept[...] = jnp.where(inside, 1.0, 0.0)
    share[...] = jnp.where(inside & (position >= start), count, 0.0)
    row = gain[...]
    prefix[...] = projected[:, 0:rows] * jnp.broadcast_to(row, (rows, features)).T
    option[...] = projected[:, rows:].T * row


def finish_kernel(
    rows, width, prefix, option, kept, share, s0, s1, s2, s3, resid_t, opt_resid,
    out_t, opt_out, summary, held_t, held_opt, held_sum, sems,
):
    squares = s0[...] + s1[...] + s2[...] + s3[...]
    scale = lax.rsqrt(squares / width + epsilon)
    held_t[...] = (resid_t[...].astype(jnp.float32) + prefix[...] * scale[:, 0:rows]).astype(
        jnp.bfloat16
    )
    copies = [
        pltpu.make_async_copy(a, b, sems.at[i])
        for i, (a, b) in enumerate(((held_t, out_t), (held_opt, opt_out), (held_sum, summary)))
    ]
    copies[0].start()
    opt = opt_resid.shape[1]
    column = jnp.broadcast_to(scale[:, rows : rows + opt], (HD, opt)).T[:, 0:1]
    full = opt_resid[0].astype(jnp.float32) + option[...] * column
    full = jnp.where(kept[:, 0:1] > 0.0, full, 0.0).astype(jnp.bfloat16)
    held_opt[0] = full
    copies[1].start()
    counts = share[:, 0:1]
    chosen = jnp.where(counts > 0.0, full.astype(jnp.float32), 0.0)
    held_sum[...] = jnp.sum(chosen, axis=0, keepdims=True) / jnp.max(counts, axis=0, keepdims=True)
    copies[2].start()
    for copy in copies:
        copy.wait()


def paired_body(
    queries,
    keys,
    values,
    prefix_resid,
    opt_queries,
    opt_keys,
    opt_values,
    opt_resid,
    out_weight,
    norm_gain,
    option_bounds,
):
    rows, opt = queries.shape[0], opt_queries.shape[1]
    features = out_weight.shape[1]
    wide = queries.shape[1] // 2
    seq = range(lax.axis_size("seq"))
    bf16, f32 = jnp.bfloat16, jnp.float32
    shape = jax.ShapeDtypeStruct
    pair = [(s, s ^ 1) for s in seq]
    first = [(s, s ^ (2 if s % 2 else 4)) for s in seq]
    second = [(s, s ^ (4 if s % 2 else 2)) for s in seq]
    both = [(s, s ^ 6) for s in seq]

    def turned(value, steps):
        count = lax.axis_size("head")
        return lax.ppermute(value, "head", [(i, (i + steps) % count) for i in range(count)])

    def after(value, *others):
        return lax.optimization_barrier((value, *others))[0]

    def in_hbm(value):
        return pltpu.with_memory_space_constraint(value, HBM)

    def crossed(value, mask):
        return lax.ppermute(value, "head", [(i, i ^ mask) for i in range(lax.axis_size("head"))])

    weight = out_weight.T

    pair_k = lax.ppermute(keys, "seq", pair)
    pair_v = lax.ppermute(values, "seq", pair)
    kept, sent = call(
        pack_kernel,
        [pltpu.VMEM((2 * rows + 2 * opt, wide), bf16), pltpu.VMEM((rows + 2 * opt, wide), bf16)],
        6,
        in_specs=[pl.BlockSpec(memory_space=HBM)] * 6,
        scratch=[pltpu.SemaphoreType.DMA((10,))],
    )(*map(in_hbm, (queries, keys, values, opt_queries, opt_keys, opt_values)))
    kv_0 = call(join_kernel, pltpu.VMEM((2 * rows, 2 * HD), bf16), 3)(kept, pair_k, pair_v)
    received = lax.ppermute(after(sent, kv_0), "seq", pair)
    kv_3 = lax.ppermute(kv_0, "seq", both)
    kv_1 = lax.ppermute(kv_0, "seq", first)
    kv_2 = lax.ppermute(kv_0, "seq", second)
    slots = (kv_0, kv_3, kv_1, kv_2)

    block = call(
        functools.partial(attn_kernel, rows, opt),
        pltpu.VMEM((2 * (rows + opt), wide), bf16),
        6,
        flops=ATTENTION_COST * 4 * (rows + opt) * wide * WINDOW,
        vmem=24,
    )(*slots, received, kept)
    block_1, block_2 = crossed(block, 1), crossed(block, 2)
    blocks = (block, block_1, block_2, crossed(block_2, 1))

    weight_1 = lax.ppermute(after(weight, kv_0), "seq", first)
    weight_2 = lax.ppermute(after(weight, block), "seq", second)
    weight_3 = lax.ppermute(after(weight_1, block), "seq", second)
    flops = 4 * features * wide * (rows + opt)
    pair_part, own_part, chosen = call(
        project_kernel,
        [shape((features, rows + opt), f32)] * 2 + [shape((features, wide), bf16)],
        6,
        flops=PROJECTION_COST * 3 * flops,
        scratch=[pltpu.VMEM((4, 2 * (rows + opt), wide), bf16)],
        vmem=16,
    )(weight, weight_1, weight_2, *blocks[:3])

    pair_part, own_part = call(
        add_kernel, [shape((features, rows + opt), f32)] * 2, 4, flops=flops, vmem=16
    )(chosen, blocks[3], pair_part, own_part)

    def complete(partial, out_shape, packed):
        return call(
            functools.partial(complete_kernel, rows, opt, packed),
            out_shape,
            6,
            flops=flops // 2,
            scratch=[pltpu.VMEM((4, rows + opt, wide), bf16)],
            vmem=16,
        )(weight_3, *blocks, partial)

    half = complete(pair_part, shape((features + features // 2, rows), bf16), True)
    received = lax.ppermute(half, "seq", pair)
    own = complete(own_part, shape((features, rows + opt), f32), False)
    projected, squares = call(
        functools.partial(square_kernel, rows, opt),
        [shape((features, rows + opt), f32), shape((1, rows + opt), f32)],
        2,
    )(own, received)
    scaled = call(
        functools.partial(scale_kernel, rows),
        [shape((features, rows), f32), shape((opt, features), f32)]
        + [shape((opt, HD), f32)] * 2,
        3,
        in_specs=[pl.BlockSpec(memory_space=SMEM)] + [pl.BlockSpec(memory_space=VMEM)] * 2,
    )(option_bounds, projected, norm_gain[None])
    results = [
        shape((features, rows), bf16),
        shape((1, opt, features), bf16),
        shape((1, features), f32),
    ]
    out_t, opt_out, summary = call(
        functools.partial(finish_kernel, rows, float(features * lax.axis_size("head"))),
        results,
        10,
        out_specs=[pl.BlockSpec(memory_space=HBM)] * 3,
        scratch=[pltpu.VMEM(r.shape, r.dtype) for r in results] + [pltpu.SemaphoreType.DMA((3,))],
    )(
        *scaled,
        squares,
        turned(squares, 1),
        turned(squares, 2),
        turned(squares, 3),
        prefix_resid.T,
        opt_resid,
    )
    return out_t.T, opt_out, summary


def body(*args):
    queries, keys, opt_queries, out_weight = args[0], args[1], args[4], args[8]
    seq, head = lax.axis_size("seq"), lax.axis_size("head")
    paired = (
        seq == 8
        and head == 4
        and seq * queries.shape[0] == WINDOW
        and queries.shape[0] == HD
        and queries.shape[0] == 2 * opt_queries.shape[1]
        and keys.shape[1] == 2 * HD
        and out_weight.shape[0] * 2 == queries.shape[1]
        and out_weight.shape[0] * seq == queries.shape[1] * head
    )
    return paired_body(*args) if paired else general_body(*args)


def solution(mesh):
    return jax.shard_map(
        body,
        mesh=mesh,
        in_specs=(
            P("seq", "head"),
            P("seq", "head"),
            P("seq", "head"),
            P("seq", "head"),
            P("seq", None, "head"),
            P("seq", None, "head"),
            P("seq", None, "head"),
            P("seq", None, "head"),
            P("seq", "head"),
            P("head"),
            P("seq", None),
        ),
        out_specs=(P("seq", "head"), P("seq", None, "head"), P("seq", "head")),
        check_vma=False,
    )
```
